32 devices in a mesh: group: 2 (over y), view: 4 (over z), depth: 2 (over x), row: 2 (over core).
Axes of the slice: x: 2, y: 2, z: 4, core: 2. Of those that a mesh axis runs over, the one named last changes fastest.
Arguments:
- features: float32 [4, 32, 8, 512], P('view', None, ('group', 'row')), parts along dimension 2, may hold values from -6 to 6
- cotangent: float32 [8, 32, 8, 512], P('depth', 'view', ('group', 'row')), parts along dimension 2, may hold values from -6 to 6
- src_row: int32 [4, 8, 8, 512], P('view', 'depth', ('group', 'row')), parts along dimension 2, may hold values from -2 to 4, as said below
- src_col: int32 [4, 8, 8, 512], P('view', 'depth', ('group', 'row')), parts along dimension 2, may hold values from 0 to 510
- fractions: int32 [2, 4, 8, 8, 512], P(None, 'view', 'depth', ('group', 'row')), parts along dimension 3, may hold values from 0 to 256
Outputs:
- grad_features: float32 [4, 32, 8, 512], P('view', None, ('group', 'row'), 'depth'), parts along dimension 2
The draws below stay inside these ranges and needn't reach their ends.
There are 2 independent parts, one for each index of `group`. The reference program is written for one: setup_inputs(seed, part) draws one part's arguments, and reference() takes and returns one part's arrays. A program takes and returns all parts, laid end to end along the dimension named above; each array names one. Nothing has to cross between parts.
Inputs may be any that keep to these rules, and one draw needn't show every extreme that they name: src_row[v, d, y, x] lies between y - 2 and y + 1.
All inputs are finite; a program needn't handle non-finite values.
Results may differ from the reference program's by a relative error of at most 0.0003.
Values sent between devices are 32-bit elements; how exact they have to be, the bound alone decides.
No kernel may reach another device: no remote copies, remote signals or barrier semaphores. Data moves between devices by JAX's collectives and lax.ppermute only.
A program may use at most 64 MiB of HBM per device.

```python
import jax
import jax.numpy as jnp
from jax import lax

C = 32
WC = 512
HALO = 2
VIEWS = 4
DEPTHS = 8
H = 4


def draw_src_row(key, part):
    shape_all = (VIEWS, DEPTHS, H, WC)
    offsets = jax.random.randint(jax.random.fold_in(key, 7), shape_all, -HALO, HALO)
    offsets = offsets.at[:, :, :, 0].set(-HALO).at[:, :, :, 1].set(HALO - 1)
    pixel_rows = lax.broadcasted_iota(jnp.int32, shape_all, 2)
    return (pixel_rows + offsets).astype(jnp.int32)


def draw_src_col(key, part):
    shape_all = (VIEWS, DEPTHS, H, WC)
    key_one, key_two = jax.random.split(jax.random.fold_in(key, 11))
    shifts = jax.random.randint(key_one, (VIEWS, 1, 1, 1), 0, 5)
    jitter = jax.random.randint(key_two, shape_all, -2, 3)
    planes = lax.broadcasted_iota(jnp.int32, shape_all, 1)
    columns = lax.broadcasted_iota(jnp.int32, shape_all, 3)
    values = jnp.clip(columns - (planes + 1) * shifts + jitter, 0, WC - 2)
    values = values.at[:, :, 0, 0].set(0).at[:, :, 0, WC - 1].set(WC - 2)
    return values.astype(jnp.int32)


def with_ends(entries, rng, least, high):
    longest = entries.shape.index(max(entries.shape))
    spots = []
    for shift in (0, 1):
        where = [jax.random.randint(jax.random.fold_in(rng, axis), (), 0, length) for axis, length in enumerate(entries.shape)]
        where[longest] = (where[longest] + shift) % entries.shape[longest]
        spots.append(tuple(where))
    return entries.at[spots[0]].set(least).at[spots[1]].set(high)


def block_levels(own_key, extent, shards, low, top_value):
    factor_of, own = 1.0, jax.random.fold_in(own_key, 6)
    for axis_at, shards_of in shards:
        heights = jnp.exp(jax.random.uniform(jax.random.fold_in(own, axis_at), (shards_of,), jnp.float32, low / len(shards), top_value / len(shards)))
        factor_of = factor_of * jnp.repeat(heights, extent[axis_at] // shards_of).reshape([-1 if axis == axis_at else 1 for axis in range(len(extent))])
    return factor_of


def scatter_about(key, shape, scale, limit, pieces=(), kind=jnp.bfloat16):
    entries = scale * jax.random.normal(key, shape, jnp.float32)
    if pieces:
        entries = entries * block_levels(key, shape, pieces, -0.22, 0.18)
    return jnp.clip(entries, -limit, limit).astype(kind)


def setup_inputs(seed: int = 0, part: int = 0) -> dict:
    key_list = jax.random.split(jax.random.key(seed), 6)
    part_keys = jax.random.split(jax.random.fold_in(key_list[5], part), 6)
    return {
        "features": scatter_about(part_keys[0], (VIEWS, C, H, WC), 1.0, 6.0, ((0, 4), (2, 2)), jnp.float32),
        "cotangent": scatter_about(part_keys[1], (DEPTHS, C, H, WC), (VIEWS / 8), 6.0, ((0, 2), (1, 4), (2, 2)), jnp.float32),
        "src_row": draw_src_row(jax.random.fold_in(jax.random.fold_in(key_list[5], part), 71), part),
        "src_col": draw_src_col(jax.random.fold_in(jax.random.fold_in(key_list[5], part), 71), part),
        "fractions": with_ends(jax.random.randint(part_keys[4], (2, VIEWS, DEPTHS, H, WC), 0, 257), jax.random.fold_in(part_keys[4], 1), 0, 256).astype(jnp.int32),
    }


def sample(flattened, flat_index, frac_row, frac_col, width):
    def corner(shift_by):
        return jnp.take(flattened, flat_index + shift_by, axis=1)
    upper_mix = (1.0 - frac_col) * corner(0) + frac_col * corner(1)
    lower_mix = (1.0 - frac_col) * corner(width) + frac_col * corner(width + 1)
    mixed = (1.0 - frac_row) * upper_mix + frac_row * lower_mix
    return jnp.transpose(mixed, (1, 0, 2, 3))


def spread(grad_warp, flat_index, frac_row, frac_col, width, length):
    moved = jnp.transpose(grad_warp, (1, 0, 2, 3))
    channels = moved.shape[0]
    upper_part = (1.0 - frac_row) * moved
    lower_part = frac_row * moved
    result = jnp.zeros((channels, length), jnp.float32)
    result = result.at[:, flat_index].add((1.0 - frac_col) * upper_part)
    result = result.at[:, flat_index + 1].add(frac_col * upper_part)
    result = result.at[:, flat_index + width].add((1.0 - frac_col) * lower_part)
    result = result.at[:, flat_index + width + 1].add(frac_col * lower_part)
    return result


def reference(features, cotangent, src_row, src_col, fractions):
    padded = jnp.pad(features, ((0, 0), (0, 0), (HALO, HALO), (0, 0)))
    length = (H + 2 * HALO) * WC
    flattened_all = padded.reshape(VIEWS, C, length)
    weights = fractions.astype(jnp.float32) / 256.0

    def warp_view(index_view):
        flat_index = ((src_row[index_view] + HALO) * WC + src_col[index_view]).astype(jnp.int32)
        warped = sample(flattened_all[index_view], flat_index, weights[0, index_view], weights[1, index_view], WC)
        return warped, flat_index

    def accumulate(index_view, running):
        return running + warp_view(index_view)[0]

    view_sum = lax.fori_loop(0, VIEWS, accumulate, jnp.zeros((DEPTHS, C, H, WC), jnp.float32))
    average = view_sum / VIEWS
    factor = 2.0 / VIEWS

    def backward_view(index_view):
        warped, flat_index = warp_view(index_view)
        grad_warp = factor * cotangent * (warped - average)
        spread_out = spread(grad_warp, flat_index, weights[0, index_view], weights[1, index_view], WC, length)
        return spread_out.reshape(C, H + 2 * HALO, WC)[:, HALO:HALO + H]

    return lax.map(backward_view, jnp.arange(VIEWS, dtype=jnp.int32))
```

```python
import functools

import jax
import jax.numpy as jnp
from jax import lax
from jax.experimental import pallas as pl
from jax.experimental.pallas import tpu as pltpu
from jax.sharding import PartitionSpec as P

HALO = 2
BF = jnp.bfloat16
F32 = jnp.float32
VMEM = pl.BlockSpec(memory_space=pltpu.VMEM)


def peer(me, k, count):
    if count & (count - 1) == 0:
        return lax.bitwise_xor(me, jnp.int32(k))
    return lax.rem(me + k, jnp.int32(count))


def pairs_of(count, k):
    if count & (count - 1) == 0:
        return [(i, i ^ k) for i in range(count)]
    return [(i, (i + k) % count) for i in range(count)]


def to_peer(block, axis, k):
    return lax.ppermute(block, axis, pairs_of(lax.axis_size(axis), k))


def to_origin(block, axis, k):
    return lax.ppermute(block, axis, [(b, a) for a, b in pairs_of(lax.axis_size(axis), k)])


def call(body, out_shape, *args, scratch=(), flops=0):
    moved = sum(a.size * 4 for a in args)
    many = isinstance(out_shape, (tuple, list))
    return pl.pallas_call(
        body,
        out_shape=out_shape,
        in_specs=[VMEM] * len(args),
        out_specs=[VMEM] * len(out_shape) if many else VMEM,
        scratch_shapes=scratch,
        cost_estimate=pl.CostEstimate(flops=flops, bytes_accessed=moved, transcendentals=0),
        compiler_params=pltpu.CompilerParams(vmem_limit_bytes=48 << 20),
    )(*args)


def pack_kernel(views, share, feat_ref, row_ref, col_ref, frac_ref, *outs):
    me = lax.axis_index("view")
    planes, rows = row_ref.shape[1:3]
    first = lax.axis_index("row") * rows
    width = feat_ref.shape[3]
    lanes = outs[0].shape[1]
    for k in range(views):
        base = peer(me, k, views) * share
        for y in range(rows):
            if share % 8:
                outs[k][y] = jnp.zeros((lanes, width), F32)
            for c in range(share):
                outs[k][y, c : c + 1, :] = feat_ref[0, base + c, y : y + 1, :]
        for d in range(planes):
            for y in range(rows):
                at = d * rows + y
                page, line = divmod(at, lanes)
                pages = -(-planes * rows // lanes)
                top = (row_ref[0, d, y : y + 1, :] - (first + y - HALO)).astype(F32)
                col = col_ref[0, d, y : y + 1, :].astype(F32)
                fy = frac_ref[0, 0, d, y : y + 1, :].astype(F32) / 256.0
                fx = frac_ref[1, 0, d, y : y + 1, :].astype(F32) / 256.0
                for kind, value in enumerate((top, col, fy, fx)):
                    outs[k][rows + kind * pages + page, line : line + 1, :] = value


def split(x):
    high = x.astype(BF)
    return high, (x - high.astype(F32)).astype(BF)


def main_kernel(views, planes, rows, share, *refs):
    packets, halo_ref, cot_ref = refs[:views], refs[views], refs[views + 1]
    own_ref, rim_ref, grad_ref, w_ref, f_ref = refs[views + 2 :]
    lanes, width = packets[0].shape[1:]
    pages = -(-planes * rows // lanes)
    padded = rows + 2 * HALO
    window = 2 * HALO + 1
    is_first = lax.axis_index("row") == 0
    for v in range(views):
        for r in range(padded):
            if r < HALO:
                x = jnp.where(is_first, 0.0, halo_ref[v, rows - HALO + r])
            elif r < HALO + rows:
                x = packets[v][r - HALO]
            else:
                x = jnp.where(is_first, halo_ref[v, r - HALO - rows], 0.0)
            f_ref[v, 2 * lanes * r : 2 * lanes * (r + 1)] = jnp.concatenate(split(x), axis=0)
    grad_ref[...] = jnp.zeros_like(grad_ref)
    block = 256

    def plane(d, carry):
        for y in range(rows):
            page, line = (d * rows + y) // lanes, (d * rows + y) % lanes
            warped, row_weights = [], []
            for v in range(views):
                top, col, fy, fx = (
                    packets[v][rows + kind * pages + page, pl.ds(line, 1), :] for kind in range(4)
                )
                left, right = (1.0 - fx).astype(BF), fx.astype(BF)
                for start in range(0, width, block):
                    it = lax.broadcasted_iota(jnp.int32, (block, width), 0).astype(F32).astype(BF)
                    here = jnp.clip(col - start, -2.0, float(block)).astype(BF)
                    after = jnp.clip(col - (start - 1), -2.0, float(block)).astype(BF)
                    w_ref[v, start : start + block, :] = jnp.where(
                        it == here, left, jnp.where(it == after, right, jnp.zeros((), BF))
                    )
                a = f_ref[v, 2 * lanes * y : 2 * lanes * (y + window)]
                p = jnp.dot(a, w_ref[v], preferred_element_type=F32)
                rw = [
                    jnp.where(top == i, 1.0 - fy, jnp.where(top == i - 1, fy, 0.0))
                    for i in range(window)
                ]
                total = 0.0
                for i in range(window):
                    at = 2 * lanes * i
                    total = total + rw[i] * (p[at : at + lanes] + p[at + lanes : at + 2 * lanes])
                warped.append(total)
                row_weights.append(rw)
            average = sum(warped) / views
            cot = cot_ref[d, :, y, :]
            if share % 8:
                cot = jnp.broadcast_to(cot, (lanes, width)) if share == 1 else jnp.pad(cot, ((0, lanes - share), (0, 0)))
            for v in range(views):
                g = (2.0 / views) * cot * (warped[v] - average)
                parts = []
                for i in range(window):
                    parts += split(row_weights[v][i] * g)
                p = lax.dot_general(
                    jnp.concatenate(parts, axis=0),
                    w_ref[v],
                    (((1,), (1,)), ((), ())),
                    preferred_element_type=F32,
                )
                for i in range(window):
                    at = 2 * lanes * i
                    grad_ref[v, y + i] += p[at : at + lanes] + p[at + lanes : at + 2 * lanes]
        return carry

    lax.fori_loop(0, planes, plane, 0, unroll=views <= 8)
    for v in range(views):
        for r in range(rows):
            own_ref[v, r] = grad_ref[v, HALO + r]
        for r in range(HALO):
            rim_ref[v, r] = jnp.where(is_first, grad_ref[v, HALO + rows + r], grad_ref[v, r])


def fold_kernel(depths, own_ref, rim_ref, *outs):
    views, rows, lanes, width = own_ref.shape
    part = width // depths
    me = lax.axis_index("depth")
    for k in range(depths):
        at = pl.multiple_of(peer(me, k, depths) * part, part)
        for v in range(views):
            for r in range(rows):
                outs[k][v, r] = own_ref[v, r, :, pl.ds(at, part)]
    is_first = lax.axis_index("row") == 0
    for k in range(depths):
        at = pl.multiple_of(peer(me, k, depths) * part, part)
        for v in range(views):
            for r in range(HALO):
                upper, lower = r, rows - HALO + r
                value = rim_ref[v, r, :, pl.ds(at, part)]
                outs[k][v, upper] += jnp.where(is_first, 0.0, value)
                outs[k][v, lower] += jnp.where(is_first, value, 0.0)


def sum_kernel(depths, views, *refs):
    for v in range(views):
        total = refs[0][v]
        for k in range(1, depths):
            total = total + refs[k][v]
        refs[depths + v][...] = total


def place_kernel(views, share, *refs):
    out_ref = refs[views]
    me = lax.axis_index("view")
    rows = out_ref.shape[2]
    for k in range(views):
        base = peer(me, k, views) * share
        for c in range(share):
            for r in range(rows):
                out_ref[0, base + c, r : r + 1, :] = refs[k][r, c : c + 1, :]


def per_device(features, cotangent, src_row, src_col, fractions):
    views = lax.axis_size("view")
    depths = lax.axis_size("depth")
    channels, rows, width = features.shape[1:]
    planes, share = cotangent.shape[:2]
    lanes = -(-share // 8) * 8
    pages = -(-planes * rows // lanes)
    packet = jax.ShapeDtypeStruct((rows + 4 * pages, lanes, width), F32)
    packets = call(
        functools.partial(pack_kernel, views, share),
        [packet] * views,
        features, src_row, src_col, fractions,
    )
    packets = [packets[0]] + [to_peer(packets[k], "view", k) for k in range(1, views)]
    halo = to_peer(jnp.stack([p[:rows] for p in packets]), "row", 1)
    volume = (views, rows, lanes, width)
    own, rim = call(
        functools.partial(main_kernel, views, planes, rows, share),
        [
            jax.ShapeDtypeStruct(volume, F32),
            jax.ShapeDtypeStruct((views, HALO, lanes, width), F32),
        ],
        *packets, halo, cotangent,
        scratch=[
            pltpu.VMEM((views, rows + 2 * HALO, lanes, width), F32),
            pltpu.VMEM((views, width, width), BF),
            pltpu.VMEM((views, 2 * lanes * (rows + 2 * HALO), width), BF),
        ],
        flops=8 * views * planes * rows * width * width * 5 * lanes,
    )
    rim = to_peer(rim, "row", 1)
    part = width // depths
    halves = call(
        functools.partial(fold_kernel, depths),
        [jax.ShapeDtypeStruct((views, rows, lanes, part), F32)] * depths,
        own, rim,
    )
    halves = [halves[0]] + [to_peer(halves[k], "depth", k) for k in range(1, depths)]
    pieces = call(
        functools.partial(sum_kernel, depths, views),
        [jax.ShapeDtypeStruct((rows, lanes, part), F32)] * views,
        *halves,
    )
    order = [pieces[0]] + [to_origin(pieces[k], "view", k) for k in range(1, views)]
    return call(
        functools.partial(place_kernel, views, share),
        jax.ShapeDtypeStruct((1, channels, rows, part), F32),
        *order,
    )


def solution(mesh):
    in_specs = (
        P("view", None, ("group", "row"), None),
        P("depth", "view", ("group", "row"), None),
        P("view", "depth", ("group", "row"), None),
        P("view", "depth", ("group", "row"), None),
        P(None, "view", "depth", ("group", "row"), None),
    )
    out_specs = P("view", None, ("group", "row"), "depth")
    return jax.shard_map(
        per_device, mesh=mesh, in_specs=in_specs, out_specs=out_specs, check_vma=False
    )
```

```python
import functools

import jax
import jax.numpy as jnp
from jax import lax
from jax.experimental import pallas as pl
from jax.experimental.pallas import tpu as pltpu
from jax.sharding import PartitionSpec as P

HALO = 2
BF = jnp.bfloat16
F32 = jnp.float32
VMEM = pl.BlockSpec(memory_space=pltpu.VMEM)


def peer(me, k, count):
    if count & (count - 1) == 0:
        return lax.bitwise_xor(me, jnp.int32(k))
    return lax.rem(me + k, jnp.int32(count))


def pairs_of(count, k):
    if count & (count - 1) == 0:
        return [(i, i ^ k) for i in range(count)]
    return [(i, (i + k) % count) for i in range(count)]


def to_peer(block, axis, k):
    return lax.ppermute(block, axis, pairs_of(lax.axis_size(axis), k))


def to_origin(block, axis, k):
    return lax.ppermute(block, axis, [(b, a) for a, b in pairs_of(lax.axis_size(axis), k)])


def call(body, out_shape, *args, scratch=(), flops=0, hbm=False, after=()):
    moved = sum(a.size * 4 for a in args)
    many = isinstance(out_shape, (tuple, list))
    if hbm:
        args = [pltpu.with_memory_space_constraint(a, pltpu.HBM) for a in args]
    space = pltpu.HBM if hbm else pltpu.VMEM
    count = len(args)

    def run(*refs):
        body(*refs[:count], *refs[count + len(after) :])

    return pl.pallas_call(
        run,
        out_shape=out_shape,
        in_specs=[pl.BlockSpec(memory_space=space)] * count
        + [pl.BlockSpec(memory_space=pl.ANY)] * len(after),
        out_specs=[VMEM] * len(out_shape) if many else VMEM,
        scratch_shapes=scratch,
        cost_estimate=pl.CostEstimate(flops=flops, bytes_accessed=moved, transcendentals=0),
        compiler_params=pltpu.CompilerParams(vmem_limit_bytes=24 << 20),
    )(*args, *after)


def pack_kernel(views, share, feat_hbm, row_hbm, col_hbm, frac_hbm, *refs):
    outs = refs[:views]
    feat_ref, row_ref, col_ref, frac_ref, sems = refs[views:]
    copies = [
        pltpu.make_async_copy(source, target, sems.at[i])
        for i, (source, target) in enumerate(
            ((feat_hbm, feat_ref), (row_hbm, row_ref), (col_hbm, col_ref), (frac_hbm, frac_ref))
        )
    ]
    for copy in copies:
        copy.start()
    for copy in copies:
        copy.wait()
    me = lax.axis_index("view")
    planes, rows = row_ref.shape[1:3]
    first = lax.axis_index("row") * rows
    width = feat_ref.shape[3]
    lanes = outs[0].shape[1]
    pages = -(-planes * rows // lanes)
    for d in range(planes):
        for y in range(rows):
            page, line = divmod(d * rows + y, lanes)
            top = (row_ref[0, d, y : y + 1, :] - (first + y - HALO)).astype(F32)
            col = col_ref[0, d, y : y + 1, :].astype(F32)
            fy = frac_ref[0, 0, d, y : y + 1, :].astype(F32) / 256.0
            fx = frac_ref[1, 0, d, y : y + 1, :].astype(F32) / 256.0
            for kind, value in enumerate((top, col, fy, fx)):
                for k in range(views):
                    outs[k][rows + kind * pages + page, line : line + 1, :] = value
    for k in range(views):
        base = peer(me, k, views) * share
        for y in range(rows):
            if share % 8:
                outs[k][y] = jnp.zeros((lanes, width), F32)
            for c in range(share):
                outs[k][y, c : c + 1, :] = feat_ref[0, base + c, y : y + 1, :]


def split(x):
    high = x.astype(BF)
    return high, (x - high.astype(F32)).astype(BF)


class Sizes:
    def __init__(self, packet, planes, rows):
        self.planes, self.rows = planes, rows
        self.lanes, self.width = packet.shape[1:]
        self.pages = -(-planes * rows // self.lanes)
        self.block = 256 if self.width % 256 == 0 else self.width
        self.segments = self.width // self.block
        self.window = 2 * HALO + 1
        self.padded = rows + 2 * HALO
        self.tall = self.segments * self.window * 2 * self.lanes

    def lookups(self):
        return pltpu.VMEM((self.window + 4 + self.segments, self.pages * self.lanes, self.width), F32)

    def one_hot(self):
        return (self.rows, self.block, self.planes * self.width)


def look_up(z, packet, t_ref):
    for page in range(z.pages):
        top, col, fy, fx = (packet[z.rows + kind * z.pages + page] for kind in range(4))
        lines = slice(page * z.lanes, (page + 1) * z.lanes)
        for i in range(z.window):
            t_ref[i, lines] = jnp.where(top == i, 1.0 - fy, jnp.where(top == i - 1, fy, 0.0))
        segment = jnp.zeros_like(col)
        for j in range(1, z.segments):
            segment = segment + jnp.where(col >= float(j * z.block), 1.0, 0.0)
        local = col - segment * float(z.block)
        t_ref[z.window, lines] = local
        t_ref[z.window + 1, lines] = segment
        t_ref[z.window + 2, lines] = 1.0 - fx
        t_ref[z.window + 3, lines] = fx
        for j in range(1, z.segments):
            border = (local == float(z.block - 1)) & (segment == float(j - 1))
            t_ref[z.window + 3 + j, lines] = jnp.where(border, fx, 0.0)


def build(z, t_ref, w_ref, d, y):
    at = pl.ds(d * z.rows + y, 1)
    local = t_ref[z.window, at, :]
    here, after = local.astype(BF), (local + 1.0).astype(BF)
    left, right = t_ref[z.window + 2, at, :].astype(BF), t_ref[z.window + 3, at, :].astype(BF)
    it = lax.broadcasted_iota(jnp.int32, (z.block, z.width), 0).astype(F32).astype(BF)
    hot = jnp.where(it == here, left, jnp.where(it == after, right, jnp.zeros((), BF)))
    columns = pl.ds(pl.multiple_of(d * z.width, 128), z.width)
    w_ref[y, :, columns] = hot


def each_plane(z, unroll, step):
    if unroll:
        for d in range(z.planes):
            step(d)
    else:
        lax.fori_loop(0, z.planes, lambda d, carry: (step(d), carry)[1], 0)


def forward(z, unroll, packet, halo, warped_ref, w_ref, t_ref, f_ref, b_ref):
    is_first = lax.axis_index("row") == 0
    look_up(z, packet, t_ref)
    half = z.window * 2 * z.lanes
    for r in range(z.padded):
        if r < HALO:
            x = jnp.where(is_first, 0.0, halo[z.rows - HALO + r])
        elif r < HALO + z.rows:
            x = packet[r - HALO]
        else:
            x = jnp.where(is_first, halo[r - HALO - z.rows], 0.0)
        both = jnp.concatenate(split(x), axis=0)
        for j in range(z.segments):
            for y in range(z.rows):
                if 0 <= r - y < z.window:
                    at = j * half + (r - y) * 2 * z.lanes
                    f_ref[y, at : at + 2 * z.lanes] = both[:, j * z.block : (j + 1) * z.block]
            if j:
                b_ref[r, j - 1] = jnp.broadcast_to(x[:, j * z.block : j * z.block + 1], x.shape)

    def step(d):
        for y in range(z.rows):
            build(z, t_ref, w_ref, d, y)
            at = pl.ds(d * z.rows + y, 1)
            columns = pl.ds(pl.multiple_of(d * z.width, 128), z.width)
            p = jnp.dot(f_ref[y], w_ref[y, :, columns], preferred_element_type=F32)
            segment = t_ref[z.window + 1, at, :]
            total = 0.0
            for i in range(z.window):
                value = 0.0
                for j in range(z.segments):
                    low = j * half + i * 2 * z.lanes
                    part = p[low : low + z.lanes] + p[low + z.lanes : low + 2 * z.lanes]
                    value = jnp.where(segment == float(j), part, value)
                for j in range(1, z.segments):
                    value = value + t_ref[z.window + 3 + j, at, :] * b_ref[y + i, j - 1]
                total = total + t_ref[i, at, :] * value
            warped_ref[d, y] = total

    each_plane(z, unroll, step)


def ahead_kernel(z, unroll, keep, count, *refs):
    packets, halo = refs[:count], refs[count]
    outs = refs[count + 1 : -3 if keep else -4]
    t_ref, f_ref, b_ref = refs[-3:]
    for v in range(count):
        w_ref = outs[count + v] if keep else refs[-4]
        forward(z, unroll, packets[v], halo.at[v], outs[v], w_ref, t_ref, f_ref, b_ref)


def backward(z, unroll, share, views, packet, warped, mean_ref, cot_ref, hot, fresh, work, own_ref, rim_ref):
    t_ref, l_ref, grad_ref, e_ref = work
    is_first = lax.axis_index("row") == 0
    half = z.window * 2 * z.lanes
    look_up(z, packet, t_ref)
    e_ref[...] = jnp.zeros_like(e_ref)

    def step(d):
        for y in range(z.rows):
            if fresh:
                build(z, t_ref, hot, d, y)
            at = pl.ds(d * z.rows + y, 1)
            columns = pl.ds(pl.multiple_of(d * z.width, 128), z.width)
            cot = cot_ref[d, :, y, :]
            if share % 8:
                rows = lax.broadcasted_iota(jnp.int32, (z.lanes, z.width), 0)
                wide = jnp.zeros((z.lanes, z.width), F32)
                for c in range(share):
                    wide = jnp.where(rows == c, cot[c : c + 1], wide)
                cot = wide
            g = (2.0 / views) * cot * (warped[d, y] - mean_ref[d, y])
            parts = []
            for i in range(z.window):
                term = t_ref[i, at, :] * g
                parts += split(term)
                for j in range(1, z.segments):
                    crossing = term * t_ref[z.window + 3 + j, at, :]
                    folded = crossing[:, :128]
                    for lane in range(128, z.width, 128):
                        folded = folded + crossing[:, lane : lane + 128]
                    e_ref[y + i, j - 1] += folded
            parts = jnp.concatenate(parts, axis=0)
            segment = t_ref[z.window + 1, at, :]
            for j in range(z.segments):
                mask = jnp.where(segment == float(j), 1.0, 0.0).astype(BF)
                l_ref[y, j * half : (j + 1) * half, columns] = parts * mask

    each_plane(z, unroll, step)
    for y in range(z.rows):
        p = lax.dot_general(
            l_ref[y], hot[y], (((1,), (1,)), ((), ())), preferred_element_type=F32
        )
        for i in range(z.window):
            for j in range(z.segments):
                low = j * half + i * 2 * z.lanes
                part = p[low : low + z.lanes] + p[low + z.lanes : low + 2 * z.lanes]
                columns = slice(j * z.block, (j + 1) * z.block)
                if y and i < z.window - 1:
                    grad_ref[y + i, :, columns] += part
                else:
                    grad_ref[y + i, :, columns] = part
    for r in range(z.padded):
        for j in range(1, z.segments):
            extra = jnp.sum(e_ref[r, j - 1], axis=1, keepdims=True)
            lane = lax.broadcasted_iota(jnp.int32, (z.lanes, 128), 1)
            columns = slice(j * z.block, j * z.block + 128)
            grad_ref[r, :, columns] += jnp.where(lane == 0, extra, 0.0)
    for r in range(z.rows):
        own_ref[r] = grad_ref[HALO + r]
    for r in range(HALO):
        rim_ref[r] = jnp.where(is_first, grad_ref[HALO + z.rows + r], grad_ref[r])


def turn_kernel(z, unroll, keep, share, views, late, count, *refs):
    early, hots_in = views - late, (count - late if keep else 0)
    packets, refs = refs[:count], refs[count:]
    halo, cot_ref, refs = refs[0], refs[1], refs[2:]
    ahead, refs = refs[:early], refs[early:]
    hots, refs = refs[:hots_in], refs[hots_in:]
    own_ref, rim_ref, mean_ref, warped_ref, w_ref, t_ref, f_ref, b_ref, l_ref, grad_ref, e_ref = refs
    for v in range(late):
        hot = w_ref.at[v if keep else 0]
        packet = packets[count - late + v]
        forward(z, unroll, packet, halo.at[v], warped_ref.at[v], hot, t_ref.at[0], f_ref, b_ref)
    warped = list(ahead) + [warped_ref.at[v] for v in range(late)]

    def average(d):
        for y in range(z.rows):
            mean_ref[d, y] = sum(w[d, y] for w in warped) / views

    each_plane(z, unroll, average)
    for v in reversed(range(count)):
        hot = w_ref.at[0]
        if keep:
            hot = hots[v] if v < count - late else w_ref.at[v - (count - late)]
        work = t_ref.at[v % 2], l_ref.at[v % 2], grad_ref.at[v % 2], e_ref.at[v % 2]
        backward(
            z, unroll, share, views, packets[v], warped[views - count + v], mean_ref, cot_ref, hot,
            not keep, work, own_ref.at[v], rim_ref.at[v],
        )


def rest_kernel(z, unroll, keep, share, views, count, *refs):
    packets, cot_ref, mean_ref, refs = refs[:count], refs[count], refs[count + 1], refs[count + 2 :]
    warped, refs = refs[:count], refs[count:]
    if keep:
        hots, refs = refs[:count], refs[count:]
    own_ref, rim_ref = refs[:2]
    t_ref, l_ref, grad_ref, e_ref = refs[-4:]
    for v in reversed(range(count)):
        work = t_ref.at[v % 2], l_ref.at[v % 2], grad_ref.at[v % 2], e_ref.at[v % 2]
        backward(
            z, unroll, share, views, packets[v], warped[v], mean_ref, cot_ref,
            hots[v] if keep else refs[2].at[0], not keep, work, own_ref.at[v], rim_ref.at[v],
        )


def stack_kernel(count, *refs):
    for v in range(count):
        refs[count][v] = refs[v][...]


def copy_kernel(in_ref, out_ref):
    out_ref[...] = in_ref[...]


def rows_kernel(count, *refs):
    rows = refs[count].shape[1]
    for v in range(count):
        refs[count][v] = refs[v][:rows]


def fold_kernel(depths, own_ref, rim_ref, *outs):
    views, rows, lanes, width = own_ref.shape
    part = width // depths
    me = lax.axis_index("depth")
    for k in range(depths):
        at = pl.multiple_of(peer(me, k, depths) * part, part)
        for v in range(views):
            for r in range(rows):
                outs[k][v, r] = own_ref[v, r, :, pl.ds(at, part)]
    is_first = lax.axis_index("row") == 0
    for k in range(depths):
        at = pl.multiple_of(peer(me, k, depths) * part, part)
        for v in range(views):
            for r in range(HALO):
                upper, lower = r, rows - HALO + r
                value = rim_ref[v, r, :, pl.ds(at, part)]
                outs[k][v, upper] += jnp.where(is_first, 0.0, value)
                outs[k][v, lower] += jnp.where(is_first, value, 0.0)


def sum_kernel(depths, views, *refs):
    for v in range(views):
        total = refs[0][v]
        for k in range(1, depths):
            total = total + refs[k][v]
        refs[depths + v][...] = total


def place_kernel(views, share, *refs):
    near, out_ref = len(refs) - 2, refs[-1]
    me = lax.axis_index("view")
    rows = out_ref.shape[2]
    for k in range(views):
        piece = refs[k] if k < near else refs[near].at[k - near]
        base = peer(me, k, views) * share
        for c in range(share):
            for r in range(rows):
                out_ref[0, base + c, r : r + 1, :] = piece[r, c : c + 1, :]


def per_device(features, cotangent, src_row, src_col, fractions):
    views = lax.axis_size("view")
    depths = lax.axis_size("depth")
    channels, rows, width = features.shape[1:]
    planes, share = cotangent.shape[:2]
    lanes = -(-share // 8) * 8
    pages = -(-planes * rows // lanes)
    packet = jax.ShapeDtypeStruct((rows + 4 * pages, lanes, width), F32)
    packets = call(
        functools.partial(pack_kernel, views, share),
        [packet] * views,
        features, src_row, src_col, fractions,
        scratch=[
            pltpu.VMEM(a.shape, a.dtype) for a in (features, src_row, src_col, fractions)
        ] + [pltpu.SemaphoreType.DMA((4,))],
        hbm=True,
    )
    packets = list(packets)
    z = Sizes(packet, planes, rows)
    keep = unroll = views <= 4
    if views <= 4:
        groups = [[k] for k in range(views)]
    else:
        groups = [[0], list(range(1, views // 2)), list(range(views // 2, views - 1)), [views - 1]]
    late = len(groups[-1])
    hot = jax.ShapeDtypeStruct(z.one_hot(), BF)
    warp = jax.ShapeDtypeStruct((planes, rows, lanes, width), F32)
    tables = [
        z.lookups(),
        pltpu.VMEM((rows, z.tall, z.block), BF),
        pltpu.VMEM((z.padded, max(z.segments - 1, 1), lanes, width), F32),
    ]
    flops = 2 * planes * rows * width * z.block * z.tall

    def halo_of(group, after=()):
        own_rows = call(
            functools.partial(rows_kernel, len(group)),
            jax.ShapeDtypeStruct((len(group), rows, lanes, width), F32),
            *[packets[k] for k in group],
            after=after,
        )
        return own_rows, to_peer(own_rows, "row", 1)

    def ahead(group, halo, after=()):
        count = len(group)
        results = call(
            functools.partial(ahead_kernel, z, unroll, keep, count),
            [warp] * count + ([hot] * count if keep else []),
            *[packets[k] for k in group], halo,
            scratch=([] if keep else [pltpu.VMEM(hot.shape, BF)]) + tables,
            flops=flops * count,
            after=after,
        )
        return results[:count], results[count:]

    halos = [halo_of(groups[0])]
    for k in range(views - 1, 0, -1):
        packets[k] = to_peer(packets[k], "view", k)
    halos.append(halo_of(groups[1]))
    warped, hots = ahead(groups[0], halos[0][1], (halos[1][0],))
    for at in range(1, len(groups) - 1):
        if at == len(groups) - 2:
            halos.append(halo_of(groups[at + 1], warped[-1:]))
            after = (halos[at + 1][0],)
        else:
            after = ()
        more, more_hots = ahead(groups[at], halos[at][1], after)
        warped, hots = warped + more, hots + more_hots
        if at + 1 < len(groups) - 1:
            halos.append(halo_of(groups[at + 1], warped[-1:]))
    first = views // 2
    last = views - first
    work = [
        pltpu.VMEM((2, rows, z.tall, planes * width), BF),
        pltpu.VMEM((2, z.padded, lanes, width), F32),
        pltpu.VMEM((2, z.padded, max(z.segments - 1, 1), lanes, 128), F32),
    ]
    twice = pltpu.VMEM((2,) + z.lookups().shape, F32)

    def results_of(count):
        return [
            jax.ShapeDtypeStruct((count, rows, lanes, width), F32),
            jax.ShapeDtypeStruct((count, HALO, lanes, width), F32),
        ]

    own, rim, mean = call(
        functools.partial(turn_kernel, z, unroll, keep, share, views, late, last),
        results_of(last) + [warp],
        *packets[first:], halos[-1][1], cotangent, *warped, *hots[first:],
        scratch=[
            pltpu.VMEM((late,) + warp.shape, F32),
            pltpu.VMEM((late if keep else 1,) + hot.shape, BF),
            twice, *tables[1:], *work,
        ],
        flops=flops * (last + late),
    )
    rim = call(copy_kernel, jax.ShapeDtypeStruct(rim.shape, F32), rim)
    own_rest, rim_rest = call(
        functools.partial(rest_kernel, z, unroll, keep, share, views, first),
        results_of(first),
        *packets[:first], cotangent, mean, *warped[:first], *hots[:first],
        scratch=([] if keep else [pltpu.VMEM((1,) + hot.shape, BF)]) + [twice, *work],
        flops=flops * first,
        after=(rim,),
    )
    part = width // depths
    pieces = []
    for own, rim in ((own, rim), (own_rest, rim_rest)):
        count = own.shape[0]
        rim = to_peer(rim, "row", 1)
        halves = call(
            functools.partial(fold_kernel, depths),
            [jax.ShapeDtypeStruct((count, rows, lanes, part), F32)] * depths,
            own, rim,
        )
        halves = [halves[0]] + [to_peer(halves[k], "depth", k) for k in range(1, depths)]
        sums = call(
            functools.partial(sum_kernel, depths, count),
            [jax.ShapeDtypeStruct((rows, lanes, part), F32)] * count,
            *halves,
        )
        pieces = list(sums) + pieces
    back = [pieces[0]] + [to_origin(pieces[k], "view", k) for k in range(1, views)]
    far = call(
        functools.partial(stack_kernel, last),
        jax.ShapeDtypeStruct((last, rows, lanes, part), F32),
        *back[first:],
    )
    return call(
        functools.partial(place_kernel, views, share),
        jax.ShapeDtypeStruct((1, channels, rows, part), F32),
        *back[:first], far,
    )


def solution(mesh):
    in_specs = (
        P("view", None, ("group", "row"), None),
        P("depth", "view", ("group", "row"), None),
        P("view", "depth", ("group", "row"), None),
        P("view", "depth", ("group", "row"), None),
        P(None, "view", "depth", ("group", "row"), None),
    )
    out_specs = P("view", None, ("group", "row"), "depth")
    return jax.shard_map(
        per_device, mesh=mesh, in_specs=in_specs, out_specs=out_specs, check_vma=False
    )
```

```python
import functools

import jax
import jax.numpy as jnp
from jax import lax
from jax.experimental import pallas as pl
from jax.experimental.pallas import tpu as pltpu
from jax.sharding import PartitionSpec as P

HALO = 2
BF = jnp.bfloat16
F32 = jnp.float32
VMEM = pl.BlockSpec(memory_space=pltpu.VMEM)


def peer(me, k, count):
    if count & (count - 1) == 0:
        return lax.bitwise_xor(me, jnp.int32(k))
    return lax.rem(me + k, jnp.int32(count))


def pairs_of(count, k):
    if count & (count - 1) == 0:
        return [(i, i ^ k) for i in range(count)]
    return [(i, (i + k) % count) for i in range(count)]


def to_peer(block, axis, k):
    return lax.ppermute(block, axis, pairs_of(lax.axis_size(axis), k))


def to_origin(block, axis, k):
    return lax.ppermute(block, axis, [(b, a) for a, b in pairs_of(lax.axis_size(axis), k)])


def call(body, out_shape, *args, scratch=(), flops=0, hbm=False, after=()):
    moved = sum(a.size * 4 for a in args)
    many = isinstance(out_shape, (tuple, list))
    if hbm:
        args = [pltpu.with_memory_space_constraint(a, pltpu.HBM) for a in args]
    space = pltpu.HBM if hbm else pltpu.VMEM
    count = len(args)

    def run(*refs):
        body(*refs[:count], *refs[count + len(after) :])

    return pl.pallas_call(
        run,
        out_shape=out_shape,
        in_specs=[pl.BlockSpec(memory_space=space)] * count
        + [pl.BlockSpec(memory_space=pl.ANY)] * len(after),
        out_specs=[VMEM] * len(out_shape) if many else VMEM,
        scratch_shapes=scratch,
        cost_estimate=pl.CostEstimate(flops=flops, bytes_accessed=moved, transcendentals=0),
        compiler_params=pltpu.CompilerParams(vmem_limit_bytes=24 << 20),
    )(*args, *after)


def pack_kernel(views, share, feat_hbm, row_hbm, col_hbm, frac_hbm, *refs):
    outs = refs[:views]
    feat_ref, row_ref, col_ref, frac_ref, sems = refs[views:]
    copies = [
        pltpu.make_async_copy(source, target, sems.at[i])
        for i, (source, target) in enumerate(
            ((feat_hbm, feat_ref), (row_hbm, row_ref), (col_hbm, col_ref), (frac_hbm, frac_ref))
        )
    ]
    for copy in copies:
        copy.start()
    for copy in copies:
        copy.wait()
    me = lax.axis_index("view")
    planes, rows = row_ref.shape[1:3]
    first = lax.axis_index("row") * rows
    width = feat_ref.shape[3]
    lanes = outs[0].shape[1]
    pages = -(-planes * rows // lanes)
    for d in range(planes):
        for y in range(rows):
            page, line = divmod(d * rows + y, lanes)
            top = (row_ref[0, d, y : y + 1, :] - (first + y - HALO)).astype(F32)
            col = col_ref[0, d, y : y + 1, :].astype(F32)
            fy = frac_ref[0, 0, d, y : y + 1, :].astype(F32) / 256.0
            fx = frac_ref[1, 0, d, y : y + 1, :].astype(F32) / 256.0
            for kind, value in enumerate((top, col, fy, fx)):
                for k in range(views):
                    outs[k][rows + kind * pages + page, line : line + 1, :] = value
    for k in range(views):
        base = peer(me, k, views) * share
        for y in range(rows):
            if share % 8:
                outs[k][y] = jnp.zeros((lanes, width), F32)
            for c in range(share):
                outs[k][y, c : c + 1, :] = feat_ref[0, base + c, y : y + 1, :]


def split(x):
    high = x.astype(BF)
    return high, (x - high.astype(F32)).astype(BF)


class Sizes:
    def __init__(self, packet, planes, rows):
        self.planes, self.rows = planes, rows
        self.lanes, self.width = packet.shape[1:]
        self.pages = -(-planes * rows // self.lanes)
        self.block = 256 if self.width % 256 == 0 else self.width
        self.segments = self.width // self.block
        self.window = 2 * HALO + 1
        self.padded = rows + 2 * HALO
        self.tall = self.segments * self.window * 2 * self.lanes

    def lookups(self):
        return pltpu.VMEM((self.window + 4 + self.segments, self.pages * self.lanes, self.width), F32)

    def one_hot(self, turned=False):
        length = self.planes * self.width
        return (self.rows,) + ((length, self.block) if turned else (self.block, length))


def look_up(z, packet, t_ref):
    for page in range(z.pages):
        top, col, fy, fx = (packet[z.rows + kind * z.pages + page] for kind in range(4))
        lines = slice(page * z.lanes, (page + 1) * z.lanes)
        for i in range(z.window):
            t_ref[i, lines] = jnp.where(top == i, 1.0 - fy, jnp.where(top == i - 1, fy, 0.0))
        segment = jnp.zeros_like(col)
        for j in range(1, z.segments):
            segment = segment + jnp.where(col >= float(j * z.block), 1.0, 0.0)
        local = col - segment * float(z.block)
        t_ref[z.window, lines] = local
        t_ref[z.window + 1, lines] = segment
        t_ref[z.window + 2, lines] = 1.0 - fx
        t_ref[z.window + 3, lines] = fx
        for j in range(1, z.segments):
            border = (local == float(z.block - 1)) & (segment == float(j - 1))
            t_ref[z.window + 3 + j, lines] = jnp.where(border, fx, 0.0)


def build(z, t_ref, w_ref, d, y):
    at = pl.ds(d * z.rows + y, 1)
    local = t_ref[z.window, at, :]
    here, after = local.astype(BF), (local + 1.0).astype(BF)
    left, right = t_ref[z.window + 2, at, :].astype(BF), t_ref[z.window + 3, at, :].astype(BF)
    it = lax.broadcasted_iota(jnp.int32, (z.block, z.width), 0).astype(F32).astype(BF)
    hot = jnp.where(it == here, left, jnp.where(it == after, right, jnp.zeros((), BF)))
    columns = pl.ds(pl.multiple_of(d * z.width, 128), z.width)
    w_ref[y, :, columns] = hot


def each_plane(z, unroll, step):
    if unroll:
        for d in range(z.planes):
            step(d)
    else:
        lax.fori_loop(0, z.planes, lambda d, carry: (step(d), carry)[1], 0)


def forward(z, unroll, packet, halo, warped_ref, w_ref, t_ref, f_ref, b_ref):
    is_first = lax.axis_index("row") == 0
    look_up(z, packet, t_ref)
    half = z.window * 2 * z.lanes
    for r in range(z.padded):
        if r < HALO:
            x = jnp.where(is_first, 0.0, halo[z.rows - HALO + r])
        elif r < HALO + z.rows:
            x = packet[r - HALO]
        else:
            x = jnp.where(is_first, halo[r - HALO - z.rows], 0.0)
        both = jnp.concatenate(split(x), axis=0)
        for j in range(z.segments):
            for y in range(z.rows):
                if 0 <= r - y < z.window:
                    at = j * half + (r - y) * 2 * z.lanes
                    f_ref[y, at : at + 2 * z.lanes] = both[:, j * z.block : (j + 1) * z.block]
            if j:
                b_ref[r, j - 1] = jnp.broadcast_to(x[:, j * z.block : j * z.block + 1], x.shape)

    def step(d):
        for y in range(z.rows):
            build(z, t_ref, w_ref, d, y)
            at = pl.ds(d * z.rows + y, 1)
            columns = pl.ds(pl.multiple_of(d * z.width, 128), z.width)
            p = jnp.dot(f_ref[y], w_ref[y, :, columns], preferred_element_type=F32)
            segment = t_ref[z.window + 1, at, :]
            total = 0.0
            for i in range(z.window):
                value = 0.0
                for j in range(z.segments):
                    low = j * half + i * 2 * z.lanes
                    part = p[low : low + z.lanes] + p[low + z.lanes : low + 2 * z.lanes]
                    value = jnp.where(segment == float(j), part, value)
                for j in range(1, z.segments):
                    value = value + t_ref[z.window + 3 + j, at, :] * b_ref[y + i, j - 1]
                total = total + t_ref[i, at, :] * value
            warped_ref[d, y] = total

    each_plane(z, unroll, step)


def ahead_kernel(z, unroll, keep, turned, count, *refs):
    packets, halo = refs[:count], refs[count]
    own_hot = turned or not keep
    outs = refs[count + 1 : -4 if own_hot else -3]
    t_ref, f_ref, b_ref = refs[-3:]
    for v in range(count):
        w_ref = refs[-4] if own_hot else outs[count + v]
        forward(z, unroll, packets[v], halo.at[v], outs[v], w_ref, t_ref, f_ref, b_ref)
        if turned:
            for y in range(z.rows):
                outs[count + v][y] = w_ref[y].T


def backward(z, unroll, share, views, packet, warped, mean_ref, cot_ref, hot, fresh, turned, work, own_ref, rim_ref):
    t_ref, l_ref, grad_ref, e_ref = work
    is_first = lax.axis_index("row") == 0
    half = z.window * 2 * z.lanes
    look_up(z, packet, t_ref)
    e_ref[...] = jnp.zeros_like(e_ref)

    def step(d):
        for y in range(z.rows):
            if fresh:
                build(z, t_ref, hot, d, y)
            at = pl.ds(d * z.rows + y, 1)
            columns = pl.ds(pl.multiple_of(d * z.width, 128), z.width)
            cot = cot_ref[d, :, y, :]
            if share % 8:
                rows = lax.broadcasted_iota(jnp.int32, (z.lanes, z.width), 0)
                wide = jnp.zeros((z.lanes, z.width), F32)
                for c in range(share):
                    wide = jnp.where(rows == c, cot[c : c + 1], wide)
                cot = wide
            g = (2.0 / views) * cot * (warped[d, y] - mean_ref[d, y])
            parts = []
            for i in range(z.window):
                term = t_ref[i, at, :] * g
                parts += split(term)
                for j in range(1, z.segments):
                    crossing = term * t_ref[z.window + 3 + j, at, :]
                    folded = crossing[:, :128]
                    for lane in range(128, z.width, 128):
                        folded = folded + crossing[:, lane : lane + 128]
                    e_ref[y + i, j - 1] += folded
            parts = jnp.concatenate(parts, axis=0)
            segment = t_ref[z.window + 1, at, :]
            for j in range(z.segments):
                mask = jnp.where(segment == float(j), 1.0, 0.0).astype(BF)
                l_ref[y, j * half : (j + 1) * half, columns] = parts * mask

    each_plane(z, unroll, step)
    for y in range(z.rows):
        p = lax.dot_general(
            l_ref[y], hot[y], (((1,), (0 if turned else 1,)), ((), ())), preferred_element_type=F32
        )
        for i in range(z.window):
            for j in range(z.segments):
                low = j * half + i * 2 * z.lanes
                part = p[low : low + z.lanes] + p[low + z.lanes : low + 2 * z.lanes]
                columns = slice(j * z.block, (j + 1) * z.block)
                if y and i < z.window - 1:
                    grad_ref[y + i, :, columns] += part
                else:
                    grad_ref[y + i, :, columns] = part
    for r in range(z.padded):
        for j in range(1, z.segments):
            extra = jnp.sum(e_ref[r, j - 1], axis=1, keepdims=True)
            lane = lax.broadcasted_iota(jnp.int32, (z.lanes, 128), 1)
            columns = slice(j * z.block, j * z.block + 128)
            grad_ref[r, :, columns] += jnp.where(lane == 0, extra, 0.0)
    for r in range(z.rows):
        own_ref[r] = grad_ref[HALO + r]
    for r in range(HALO):
        rim_ref[r] = jnp.where(is_first, grad_ref[HALO + z.rows + r], grad_ref[r])


def turn_kernel(z, unroll, keep, share, views, late, count, *refs):
    early, hots_in = views - late, (count - late if keep else 0)
    packets, refs = refs[:count], refs[count:]
    halo, cot_ref, refs = refs[0], refs[1], refs[2:]
    ahead, refs = refs[:early], refs[early:]
    hots, refs = refs[:hots_in], refs[hots_in:]
    own_ref, rim_ref, mean_ref, warped_ref, w_ref, t_ref, f_ref, b_ref, l_ref, grad_ref, e_ref = refs
    for v in range(late):
        hot = w_ref.at[v if keep else 0]
        packet = packets[count - late + v]
        forward(z, unroll, packet, halo.at[v], warped_ref.at[v], hot, t_ref.at[0], f_ref, b_ref)
    warped = list(ahead) + [warped_ref.at[v] for v in range(late)]

    def average(d):
        for y in range(z.rows):
            mean_ref[d, y] = sum(w[d, y] for w in warped) / views

    each_plane(z, unroll, average)
    for v in reversed(range(count)):
        hot = w_ref.at[0]
        if keep:
            hot = hots[v] if v < count - late else w_ref.at[v - (count - late)]
        work = t_ref.at[v % 2], l_ref.at[v % 2], grad_ref.at[v % 2], e_ref.at[v % 2]
        backward(
            z, unroll, share, views, packets[v], warped[views - count + v], mean_ref, cot_ref, hot,
            not keep, keep and hot.shape != w_ref.at[0].shape, work, own_ref.at[v], rim_ref.at[v],
        )


def rest_kernel(z, unroll, keep, share, views, count, *refs):
    packets, cot_ref, mean_ref, refs = refs[:count], refs[count], refs[count + 1], refs[count + 2 :]
    warped, refs = refs[:count], refs[count:]
    if keep:
        hots, refs = refs[:count], refs[count:]
    own_ref, rim_ref = refs[:2]
    t_ref, l_ref, grad_ref, e_ref = refs[-4:]
    for v in reversed(range(count)):
        work = t_ref.at[v % 2], l_ref.at[v % 2], grad_ref.at[v % 2], e_ref.at[v % 2]
        backward(
            z, unroll, share, views, packets[v], warped[v], mean_ref, cot_ref,
            hots[v] if keep else refs[2].at[0], not keep, False, work, own_ref.at[v], rim_ref.at[v],
        )


def stack_kernel(count, *refs):
    for v in range(count):
        refs[count][v] = refs[v][...]


def copy_kernel(in_ref, out_ref):
    out_ref[...] = in_ref[...]


def rows_kernel(count, *refs):
    rows = refs[count].shape[1]
    for v in range(count):
        refs[count][v] = refs[v][:rows]


def fold_kernel(depths, own_ref, rim_ref, *outs):
    views, rows, lanes, width = own_ref.shape
    part = width // depths
    me = lax.axis_index("depth")
    for k in range(depths):
        at = pl.multiple_of(peer(me, k, depths) * part, part)
        for v in range(views):
            for r in range(rows):
                outs[k][v, r] = own_ref[v, r, :, pl.ds(at, part)]
    is_first = lax.axis_index("row") == 0
    for k in range(depths):
        at = pl.multiple_of(peer(me, k, depths) * part, part)
        for v in range(views):
            for r in range(HALO):
                upper, lower = r, rows - HALO + r
                value = rim_ref[v, r, :, pl.ds(at, part)]
                outs[k][v, upper] += jnp.where(is_first, 0.0, value)
                outs[k][v, lower] += jnp.where(is_first, value, 0.0)


def sum_kernel(depths, views, *refs):
    for v in range(views):
        total = refs[0][v]
        for k in range(1, depths):
            total = total + refs[k][v]
        refs[depths + v][...] = total


def place_kernel(views, share, *refs):
    near, out_ref = len(refs) - 2, refs[-1]
    me = lax.axis_index("view")
    rows = out_ref.shape[2]
    for k in range(views):
        piece = refs[k] if k < near else refs[near].at[views - 1 - k]
        base = peer(me, k, views) * share
        for c in range(share):
            for r in range(rows):
                out_ref[0, base + c, r : r + 1, :] = piece[r, c : c + 1, :]


def per_device(features, cotangent, src_row, src_col, fractions):
    views = lax.axis_size("view")
    depths = lax.axis_size("depth")
    channels, rows, width = features.shape[1:]
    planes, share = cotangent.shape[:2]
    lanes = -(-share // 8) * 8
    pages = -(-planes * rows // lanes)
    packet = jax.ShapeDtypeStruct((rows + 4 * pages, lanes, width), F32)
    packets = call(
        functools.partial(pack_kernel, views, share),
        [packet] * views,
        features, src_row, src_col, fractions,
        scratch=[
            pltpu.VMEM(a.shape, a.dtype) for a in (features, src_row, src_col, fractions)
        ] + [pltpu.SemaphoreType.DMA((4,))],
        hbm=True,
    )
    packets = list(packets)
    z = Sizes(packet, planes, rows)
    keep = unroll = views <= 4
    if views <= 4:
        groups = [[k] for k in range(views)]
    else:
        groups = [[0], list(range(1, views // 2)), list(range(views // 2, views - 1)), [views - 1]]
    late = len(groups[-1])
    hot = jax.ShapeDtypeStruct(z.one_hot(), BF)
    warp = jax.ShapeDtypeStruct((planes, rows, lanes, width), F32)
    tables = [
        z.lookups(),
        pltpu.VMEM((rows, z.tall, z.block), BF),
        pltpu.VMEM((z.padded, max(z.segments - 1, 1), lanes, width), F32),
    ]
    flops = 2 * planes * rows * width * z.block * z.tall

    def halo_of(group, after=()):
        own_rows = call(
            functools.partial(rows_kernel, len(group)),
            jax.ShapeDtypeStruct((len(group), rows, lanes, width), F32),
            *[packets[k] for k in group],
            after=after,
        )
        return own_rows, to_peer(own_rows, "row", 1)

    def ahead(group, halo, after=(), turned=False):
        count = len(group)
        shape = jax.ShapeDtypeStruct(z.one_hot(turned), BF)
        results = call(
            functools.partial(ahead_kernel, z, unroll, keep, turned, count),
            [warp] * count + ([shape] * count if keep else []),
            *[packets[k] for k in group], halo,
            scratch=([] if keep and not turned else [pltpu.VMEM(hot.shape, BF)]) + tables,
            flops=flops * count,
            after=after,
        )
        return results[:count], results[count:]

    halos = [halo_of(groups[0])]
    for k in range(views - 1, 0, -1):
        packets[k] = to_peer(packets[k], "view", k)
    halos.append(halo_of(groups[1]))
    warped, hots = ahead(groups[0], halos[0][1], (halos[1][0],))
    for at in range(1, len(groups) - 1):
        if at == len(groups) - 2:
            halos.append(halo_of(groups[at + 1], warped[-1:]))
            after = (halos[at + 1][0],)
        else:
            after = ()
        more, more_hots = ahead(groups[at], halos[at][1], after, keep and groups[at] == [1])
        warped, hots = warped + more, hots + more_hots
        if at + 1 < len(groups) - 1:
            halos.append(halo_of(groups[at + 1], warped[-1:]))
    first = max(views // 4, 1)
    last = views - first
    work = [
        pltpu.VMEM((2, rows, z.tall, planes * width), BF),
        pltpu.VMEM((2, z.padded, lanes, width), F32),
        pltpu.VMEM((2, z.padded, max(z.segments - 1, 1), lanes, 128), F32),
    ]
    twice = pltpu.VMEM((2,) + z.lookups().shape, F32)

    def results_of(count):
        return [
            jax.ShapeDtypeStruct((count, rows, lanes, width), F32),
            jax.ShapeDtypeStruct((count, HALO, lanes, width), F32),
        ]

    own, rim, mean = call(
        functools.partial(turn_kernel, z, unroll, keep, share, views, late, last),
        results_of(last) + [warp],
        *packets[first:], halos[-1][1], cotangent, *warped, *hots[first:],
        scratch=[
            pltpu.VMEM((late,) + warp.shape, F32),
            pltpu.VMEM((late if keep else 1,) + hot.shape, BF),
            twice, *tables[1:], *work,
        ],
        flops=flops * (last + late),
    )
    rim = call(copy_kernel, jax.ShapeDtypeStruct(rim.shape, F32), rim)
    own_rest, rim_rest = call(
        functools.partial(rest_kernel, z, unroll, keep, share, views, first),
        results_of(first),
        *packets[:first], cotangent, mean, *warped[:first], *hots[:first],
        scratch=([] if keep else [pltpu.VMEM((1,) + hot.shape, BF)]) + [twice, *work],
        flops=flops * first,
        after=(rim,),
    )
    part = width // depths
    pieces = []
    for own, rim, after in ((own, rim, (own_rest,)), (own_rest, rim_rest, ())):
        count = own.shape[0]
        rim = to_peer(rim, "row", 1)
        halves = call(
            functools.partial(fold_kernel, depths),
            [jax.ShapeDtypeStruct((count, rows, lanes, part), F32)] * depths,
            own, rim,
            after=after,
        )
        halves = [halves[0]] + [to_peer(halves[k], "depth", k) for k in range(1, depths)]
        sums = call(
            functools.partial(sum_kernel, depths, count),
            [jax.ShapeDtypeStruct((rows, lanes, part), F32)] * count,
            *halves,
        )
        pieces = list(sums) + pieces
    back = [pieces[0]] + [to_origin(pieces[k], "view", k) for k in range(1, views)]
    far = call(
        functools.partial(stack_kernel, last),
        jax.ShapeDtypeStruct((last, rows, lanes, part), F32),
        *back[:first - 1 : -1],
    )
    return call(
        functools.partial(place_kernel, views, share),
        jax.ShapeDtypeStruct((1, channels, rows, part), F32),
        *back[:first], far,
    )


def solution(mesh):
    in_specs = (
        P("view", None, ("group", "row"), None),
        P("depth", "view", ("group", "row"), None),
        P("view", "depth", ("group", "row"), None),
        P("view", "depth", ("group", "row"), None),
        P(None, "view", "depth", ("group", "row"), None),
    )
    out_specs = P("view", None, ("group", "row"), "depth")
    return jax.shard_map(
        per_device, mesh=mesh, in_specs=in_specs, out_specs=out_specs, check_vma=False
    )
```

```python
import functools

import jax
import jax.numpy as jnp
from jax import lax
from jax.experimental import pallas as pl
from jax.experimental.pallas import tpu as pltpu
from jax.sharding import PartitionSpec as P

HALO = 2
BF = jnp.bfloat16
F32 = jnp.float32
VMEM = pl.BlockSpec(memory_space=pltpu.VMEM)


def peer(me, k, count):
    if count & (count - 1) == 0:
        return lax.bitwise_xor(me, jnp.int32(k))
    return lax.rem(me + k, jnp.int32(count))


def pairs_of(count, k):
    if count & (count - 1) == 0:
        return [(i, i ^ k) for i in range(count)]
    return [(i, (i + k) % count) for i in range(count)]


def to_peer(block, axis, k):
    return lax.ppermute(block, axis, pairs_of(lax.axis_size(axis), k))


def to_origin(block, axis, k):
    return lax.ppermute(block, axis, [(b, a) for a, b in pairs_of(lax.axis_size(axis), k)])


def call(body, out_shape, *args, scratch=(), flops=0, hbm=False, after=()):
    moved = sum(a.size * 4 for a in args)
    many = isinstance(out_shape, (tuple, list))
    if hbm:
        args = [pltpu.with_memory_space_constraint(a, pltpu.HBM) for a in args]
    space = pltpu.HBM if hbm else pltpu.VMEM
    count = len(args)

    def run(*refs):
        body(*refs[:count], *refs[count + len(after) :])

    return pl.pallas_call(
        run,
        out_shape=out_shape,
        in_specs=[pl.BlockSpec(memory_space=space)] * count
        + [pl.BlockSpec(memory_space=pl.ANY)] * len(after),
        out_specs=[VMEM] * len(out_shape) if many else VMEM,
        scratch_shapes=scratch,
        cost_estimate=pl.CostEstimate(flops=flops, bytes_accessed=moved, transcendentals=0),
        compiler_params=pltpu.CompilerParams(vmem_limit_bytes=24 << 20),
    )(*args, *after)


def pack_kernel(views, share, feat_hbm, row_hbm, col_hbm, frac_hbm, *refs):
    outs = refs[:views]
    feat_ref, row_ref, col_ref, frac_ref, sems = refs[views:]
    copies = [
        pltpu.make_async_copy(source, target, sems.at[i])
        for i, (source, target) in enumerate(
            ((feat_hbm, feat_ref), (row_hbm, row_ref), (col_hbm, col_ref), (frac_hbm, frac_ref))
        )
    ]
    for copy in copies:
        copy.start()
    for copy in copies:
        copy.wait()
    me = lax.axis_index("view")
    planes, rows = row_ref.shape[1:3]
    first = lax.axis_index("row") * rows
    width = feat_ref.shape[3]
    lanes = outs[0].shape[1]
    pages = -(-planes * rows // lanes)
    for d in range(planes):
        for y in range(rows):
            page, line = divmod(d * rows + y, lanes)
            top = (row_ref[0, d, y : y + 1, :] - (first + y - HALO)).astype(F32)
            col = col_ref[0, d, y : y + 1, :].astype(F32)
            fy = frac_ref[0, 0, d, y : y + 1, :].astype(F32) / 256.0
            fx = frac_ref[1, 0, d, y : y + 1, :].astype(F32) / 256.0
            for kind, value in enumerate((top, col, fy, fx)):
                for k in range(views):
                    outs[k][rows + kind * pages + page, line : line + 1, :] = value
    for k in range(views):
        base = peer(me, k, views) * share
        for y in range(rows):
            if share % 8:
                outs[k][y] = jnp.zeros((lanes, width), F32)
            for c in range(share):
                outs[k][y, c : c + 1, :] = feat_ref[0, base + c, y : y + 1, :]


def split(x):
    high = x.astype(BF)
    return high, (x - high.astype(F32)).astype(BF)


class Sizes:
    def __init__(self, packet, planes, rows):
        self.planes, self.rows = planes, rows
        self.lanes, self.width = packet.shape[1:]
        self.pages = -(-planes * rows // self.lanes)
        self.block = 256 if self.width % 256 == 0 else self.width
        self.segments = self.width // self.block
        self.window = 2 * HALO + 1
        self.padded = rows + 2 * HALO
        self.tall = self.segments * self.window * 2 * self.lanes

    def lookups(self):
        return pltpu.VMEM((self.window + 4 + self.segments, self.pages * self.lanes, self.width), F32)

    def one_hot(self, turned=False):
        length = self.planes * self.width
        return (self.rows,) + ((length, self.block) if turned else (self.block, length))


def look_up(z, packet, t_ref):
    for page in range(z.pages):
        top, col, fy, fx = (packet[z.rows + kind * z.pages + page] for kind in range(4))
        lines = slice(page * z.lanes, (page + 1) * z.lanes)
        for i in range(z.window):
            t_ref[i, lines] = jnp.where(top == i, 1.0 - fy, jnp.where(top == i - 1, fy, 0.0))
        segment = jnp.zeros_like(col)
        for j in range(1, z.segments):
            segment = segment + jnp.where(col >= float(j * z.block), 1.0, 0.0)
        local = col - segment * float(z.block)
        t_ref[z.window, lines] = local
        t_ref[z.window + 1, lines] = segment
        t_ref[z.window + 2, lines] = 1.0 - fx
        t_ref[z.window + 3, lines] = fx
        for j in range(1, z.segments):
            border = (local == float(z.block - 1)) & (segment == float(j - 1))
            t_ref[z.window + 3 + j, lines] = jnp.where(border, fx, 0.0)


def build(z, t_ref, w_ref, d, y):
    at = pl.ds(d * z.rows + y, 1)
    local = t_ref[z.window, at, :]
    here, after = local.astype(BF), (local + 1.0).astype(BF)
    left, right = t_ref[z.window + 2, at, :].astype(BF), t_ref[z.window + 3, at, :].astype(BF)
    it = lax.broadcasted_iota(jnp.int32, (z.block, z.width), 0).astype(F32).astype(BF)
    hot = jnp.where(it == here, left, jnp.where(it == after, right, jnp.zeros((), BF)))
    columns = pl.ds(pl.multiple_of(d * z.width, 128), z.width)
    w_ref[y, :, columns] = hot


def each_plane(z, unroll, step):
    if unroll:
        for d in range(z.planes):
            step(d)
    else:
        lax.fori_loop(0, z.planes, lambda d, carry: (step(d), carry)[1], 0)


def forward(z, unroll, packet, halo, warped_ref, w_ref, t_ref, f_ref, b_ref):
    is_first = lax.axis_index("row") == 0
    look_up(z, packet, t_ref)
    half = z.window * 2 * z.lanes
    for r in range(z.padded):
        if r < HALO:
            x = jnp.where(is_first, 0.0, halo[z.rows - HALO + r])
        elif r < HALO + z.rows:
            x = packet[r - HALO]
        else:
            x = jnp.where(is_first, halo[r - HALO - z.rows], 0.0)
        both = jnp.concatenate(split(x), axis=0)
        for j in range(z.segments):
            for y in range(z.rows):
                if 0 <= r - y < z.window:
                    at = j * half + (r - y) * 2 * z.lanes
                    f_ref[y, at : at + 2 * z.lanes] = both[:, j * z.block : (j + 1) * z.block]
            if j:
                b_ref[r, j - 1] = jnp.broadcast_to(x[:, j * z.block : j * z.block + 1], x.shape)

    def step(d):
        for y in range(z.rows):
            build(z, t_ref, w_ref, d, y)
            at = pl.ds(d * z.rows + y, 1)
            columns = pl.ds(pl.multiple_of(d * z.width, 128), z.width)
            p = jnp.dot(f_ref[y], w_ref[y, :, columns], preferred_element_type=F32)
            segment = t_ref[z.window + 1, at, :]
            total = 0.0
            for i in range(z.window):
                value = 0.0
                for j in range(z.segments):
                    low = j * half + i * 2 * z.lanes
                    part = p[low : low + z.lanes] + p[low + z.lanes : low + 2 * z.lanes]
                    value = jnp.where(segment == float(j), part, value)
                for j in range(1, z.segments):
                    value = value + t_ref[z.window + 3 + j, at, :] * b_ref[y + i, j - 1]
                total = total + t_ref[i, at, :] * value
            warped_ref[d, y] = total

    each_plane(z, unroll, step)


def ahead_kernel(z, unroll, keep, turned, count, *refs):
    packets, halo = refs[:count], refs[count]
    own_hot = turned or not keep
    outs = refs[count + 1 : -4 if own_hot else -3]
    t_ref, f_ref, b_ref = refs[-3:]
    for v in range(count):
        w_ref = refs[-4] if own_hot else outs[count + v]
        forward(z, unroll, packets[v], halo.at[v], outs[v], w_ref, t_ref, f_ref, b_ref)
        if turned:
            for y in range(z.rows):
                outs[count + v][y] = w_ref[y].T


def backward(z, unroll, share, views, packet, warped, mean_ref, cot_ref, hot, fresh, turned, work, own_ref, rim_ref):
    t_ref, l_ref, grad_ref, e_ref = work
    is_first = lax.axis_index("row") == 0
    half = z.window * 2 * z.lanes
    look_up(z, packet, t_ref)
    e_ref[...] = jnp.zeros_like(e_ref)

    def step(d):
        for y in range(z.rows):
            if fresh:
                build(z, t_ref, hot, d, y)
            at = pl.ds(d * z.rows + y, 1)
            columns = pl.ds(pl.multiple_of(d * z.width, 128), z.width)
            cot = cot_ref[d, :, y, :]
            if share % 8:
                rows = lax.broadcasted_iota(jnp.int32, (z.lanes, z.width), 0)
                wide = jnp.zeros((z.lanes, z.width), F32)
                for c in range(share):
                    wide = jnp.where(rows == c, cot[c : c + 1], wide)
                cot = wide
            g = (2.0 / views) * cot * (warped[d, y] - mean_ref[d, y])
            parts = []
            for i in range(z.window):
                term = t_ref[i, at, :] * g
                parts += split(term)
                for j in range(1, z.segments):
                    crossing = term * t_ref[z.window + 3 + j, at, :]
                    folded = crossing[:, :128]
                    for lane in range(128, z.width, 128):
                        folded = folded + crossing[:, lane : lane + 128]
                    e_ref[y + i, j - 1] += folded
            parts = jnp.concatenate(parts, axis=0)
            segment = t_ref[z.window + 1, at, :]
            for j in range(z.segments):
                mask = jnp.where(segment == float(j), 1.0, 0.0).astype(BF)
                l_ref[y, j * half : (j + 1) * half, columns] = parts * mask

    each_plane(z, unroll, step)
    for y in range(z.rows):
        p = lax.dot_general(
            l_ref[y], hot[y], (((1,), (0 if turned else 1,)), ((), ())), preferred_element_type=F32
        )
        for i in range(z.window):
            for j in range(z.segments):
                low = j * half + i * 2 * z.lanes
                part = p[low : low + z.lanes] + p[low + z.lanes : low + 2 * z.lanes]
                columns = slice(j * z.block, (j + 1) * z.block)
                if y and i < z.window - 1:
                    grad_ref[y + i, :, columns] += part
                else:
                    grad_ref[y + i, :, columns] = part
    for r in range(z.padded):
        for j in range(1, z.segments):
            extra = jnp.sum(e_ref[r, j - 1], axis=1, keepdims=True)
            lane = lax.broadcasted_iota(jnp.int32, (z.lanes, 128), 1)
            columns = slice(j * z.block, j * z.block + 128)
            grad_ref[r, :, columns] += jnp.where(lane == 0, extra, 0.0)
    for r in range(z.rows):
        own_ref[r] = grad_ref[HALO + r]
    for r in range(HALO):
        rim_ref[r] = jnp.where(is_first, grad_ref[HALO + z.rows + r], grad_ref[r])


def turn_kernel(z, unroll, keep, share, views, late, count, *refs):
    early, hots_in = views - late, (count - late if keep else 0)
    packets, refs = (refs[count - 1],) + refs[: count - 1], refs[count:]
    halo, cot_ref, refs = refs[0], refs[1], refs[2:]
    ahead, refs = refs[:early], refs[early:]
    hots, refs = refs[:hots_in], refs[hots_in:]
    own_ref, rim_ref, mean_ref, warped_ref, w_ref, t_ref, f_ref, b_ref, l_ref, grad_ref, e_ref = refs
    for v in range(late):
        hot = w_ref.at[v if keep else 0]
        packet = packets[count - late + v]
        forward(z, unroll, packet, halo.at[v], warped_ref.at[v], hot, t_ref.at[0], f_ref, b_ref)
    warped = list(ahead) + [warped_ref.at[v] for v in range(late)]

    def average(d):
        for y in range(z.rows):
            mean_ref[d, y] = sum(w[d, y] for w in warped) / views

    each_plane(z, unroll, average)
    for v in reversed(range(count)):
        hot = w_ref.at[0]
        if keep:
            hot = hots[v] if v < count - late else w_ref.at[v - (count - late)]
        work = t_ref.at[v % 2], l_ref.at[v % 2], grad_ref.at[v % 2], e_ref.at[v % 2]
        backward(
            z, unroll, share, views, packets[v], warped[views - count + v], mean_ref, cot_ref, hot,
            not keep, keep and hot.shape != w_ref.at[0].shape, work, own_ref.at[v], rim_ref.at[v],
        )


def rest_kernel(z, unroll, keep, share, views, count, *refs):
    packets, cot_ref, mean_ref, refs = refs[:count], refs[count], refs[count + 1], refs[count + 2 :]
    warped, refs = refs[:count], refs[count:]
    if keep:
        hots, refs = refs[:count], refs[count:]
    own_ref, rim_ref = refs[:2]
    t_ref, l_ref, grad_ref, e_ref = refs[-4:]
    for v in reversed(range(count)):
        work = t_ref.at[v % 2], l_ref.at[v % 2], grad_ref.at[v % 2], e_ref.at[v % 2]
        backward(
            z, unroll, share, views, packets[v], warped[v], mean_ref, cot_ref,
            hots[v] if keep else refs[2].at[0], not keep, False, work, own_ref.at[v], rim_ref.at[v],
        )


def stack_kernel(count, *refs):
    for v in range(count):
        refs[count][v] = refs[v][...]


def copy_kernel(in_ref, out_ref):
    out_ref[...] = in_ref[...]


def rows_kernel(count, *refs):
    rows = refs[count].shape[1]
    for v in range(count):
        refs[count][v] = refs[v][:rows]


def fold_kernel(depths, own_ref, rim_ref, *outs):
    views, rows, lanes, width = own_ref.shape
    part = width // depths
    me = lax.axis_index("depth")
    for k in range(depths):
        at = pl.multiple_of(peer(me, k, depths) * part, part)
        for v in range(views):
            for r in range(rows):
                outs[k][v, r] = own_ref[v, r, :, pl.ds(at, part)]
    is_first = lax.axis_index("row") == 0
    for k in range(depths):
        at = pl.multiple_of(peer(me, k, depths) * part, part)
        for v in range(views):
            for r in range(HALO):
                upper, lower = r, rows - HALO + r
                value = rim_ref[v, r, :, pl.ds(at, part)]
                outs[k][v, upper] += jnp.where(is_first, 0.0, value)
                outs[k][v, lower] += jnp.where(is_first, value, 0.0)


def sum_kernel(depths, views, *refs):
    for v in range(views):
        total = refs[0][v]
        for k in range(1, depths):
            total = total + refs[k][v]
        refs[depths + v][...] = total


def place_kernel(views, share, *refs):
    near, out_ref = len(refs) - 2, refs[-1]
    me = lax.axis_index("view")
    rows = out_ref.shape[2]
    for k in range(views):
        piece = refs[k + 1] if k < near else refs[0].at[views - 1 - k]
        base = peer(me, k, views) * share
        for c in range(share):
            for r in range(rows):
                out_ref[0, base + c, r : r + 1, :] = piece[r, c : c + 1, :]


def per_device(features, cotangent, src_row, src_col, fractions):
    views = lax.axis_size("view")
    depths = lax.axis_size("depth")
    channels, rows, width = features.shape[1:]
    planes, share = cotangent.shape[:2]
    lanes = -(-share // 8) * 8
    pages = -(-planes * rows // lanes)
    packet = jax.ShapeDtypeStruct((rows + 4 * pages, lanes, width), F32)
    packets = call(
        functools.partial(pack_kernel, views, share),
        [packet] * views,
        features, src_row, src_col, fractions,
        scratch=[
            pltpu.VMEM(a.shape, a.dtype) for a in (features, src_row, src_col, fractions)
        ] + [pltpu.SemaphoreType.DMA((4,))],
        hbm=True,
    )
    packets = list(packets)
    z = Sizes(packet, planes, rows)
    keep = unroll = views <= 4
    if views <= 4:
        groups = [[k] for k in range(views)]
    else:
        groups = [[0], list(range(1, views // 2)), list(range(views // 2, views - 1)), [views - 1]]
    late = len(groups[-1])
    hot = jax.ShapeDtypeStruct(z.one_hot(), BF)
    warp = jax.ShapeDtypeStruct((planes, rows, lanes, width), F32)
    tables = [
        z.lookups(),
        pltpu.VMEM((rows, z.tall, z.block), BF),
        pltpu.VMEM((z.padded, max(z.segments - 1, 1), lanes, width), F32),
    ]
    flops = 2 * planes * rows * width * z.block * z.tall

    def halo_of(group, after=()):
        own_rows = call(
            functools.partial(rows_kernel, len(group)),
            jax.ShapeDtypeStruct((len(group), rows, lanes, width), F32),
            *[packets[k] for k in group],
            after=after,
        )
        return own_rows, to_peer(own_rows, "row", 1)

    def ahead(group, halo, after=(), turned=False):
        count = len(group)
        shape = jax.ShapeDtypeStruct(z.one_hot(turned), BF)
        results = call(
            functools.partial(ahead_kernel, z, unroll, keep, turned, count),
            [warp] * count + ([shape] * count if keep else []),
            *[packets[k] for k in group], halo,
            scratch=([] if keep and not turned else [pltpu.VMEM(hot.shape, BF)]) + tables,
            flops=flops * count,
            after=after,
        )
        return results[:count], results[count:]

    own_halo = halo_of([0])[1]
    for k in range(1, views):
        packets[k] = to_peer(packets[k], "view", k)
    warped, hots = ahead([0], own_halo)
    middle = list(range(1, views - late))
    sent, middle_halo = halo_of(middle[::-1], warped)
    last_sent, last_halo = halo_of(groups[-1], (sent,))
    for k in middle:
        at = len(middle) - k
        after = (last_sent,) if k == 1 else warped[-1:]
        more, more_hots = ahead([k], middle_halo[at : at + 1], after, keep and k == 1)
        warped, hots = warped + more, hots + more_hots
    first = max(views // 4, 1)
    last = views - first
    work = [
        pltpu.VMEM((2, rows, z.tall, planes * width), BF),
        pltpu.VMEM((2, z.padded, lanes, width), F32),
        pltpu.VMEM((2, z.padded, max(z.segments - 1, 1), lanes, 128), F32),
    ]
    twice = pltpu.VMEM((2,) + z.lookups().shape, F32)

    def results_of(count):
        return [
            jax.ShapeDtypeStruct((count, rows, lanes, width), F32),
            jax.ShapeDtypeStruct((count, HALO, lanes, width), F32),
        ]

    own, rim, mean = call(
        functools.partial(turn_kernel, z, unroll, keep, share, views, late, last),
        results_of(last) + [warp],
        *packets[first + 1 :], packets[first], last_halo, cotangent, *warped, *hots[first:],
        scratch=[
            pltpu.VMEM((late,) + warp.shape, F32),
            pltpu.VMEM((late if keep else 1,) + hot.shape, BF),
            twice, *tables[1:], *work,
        ],
        flops=flops * (last + late),
    )
    rim = call(copy_kernel, jax.ShapeDtypeStruct(rim.shape, F32), rim)
    own_rest, rim_rest = call(
        functools.partial(rest_kernel, z, unroll, keep, share, views, first),
        results_of(first),
        *packets[:first], cotangent, mean, *warped[:first], *hots[:first],
        scratch=([] if keep else [pltpu.VMEM((1,) + hot.shape, BF)]) + [twice, *work],
        flops=flops * first,
        after=(rim,),
    )
    part = width // depths
    pieces = []
    for own, rim, after in ((own, rim, (own_rest,)), (own_rest, rim_rest, ())):
        count = own.shape[0]
        rim = to_peer(rim, "row", 1)
        halves = call(
            functools.partial(fold_kernel, depths),
            [jax.ShapeDtypeStruct((count, rows, lanes, part), F32)] * depths,
            own, rim,
            after=after,
        )
        halves = [halves[0]] + [to_peer(halves[k], "depth", k) for k in range(1, depths)]
        sums = call(
            functools.partial(sum_kernel, depths, count),
            [jax.ShapeDtypeStruct((rows, lanes, part), F32)] * count,
            *halves,
        )
        pieces = list(sums) + pieces
    back = [pieces[0]] + [to_origin(pieces[k], "view", k) for k in range(1, views)]
    far = call(
        functools.partial(stack_kernel, last),
        jax.ShapeDtypeStruct((last, rows, lanes, part), F32),
        *back[:first - 1 : -1],
    )
    return call(
        functools.partial(place_kernel, views, share),
        jax.ShapeDtypeStruct((1, channels, rows, part), F32),
        far, *back[:first],
    )


def solution(mesh):
    in_specs = (
        P("view", None, ("group", "row"), None),
        P("depth", "view", ("group", "row"), None),
        P("view", "depth", ("group", "row"), None),
        P("view", "depth", ("group", "row"), None),
        P(None, "view", "depth", ("group", "row"), None),
    )
    out_specs = P("view", None, ("group", "row"), "depth")
    return jax.shard_map(
        per_device, mesh=mesh, in_specs=in_specs, out_specs=out_specs, check_vma=False
    )
```

```python
import functools

import jax
import jax.numpy as jnp
from jax import lax
from jax.experimental import pallas as pl
from jax.experimental.pallas import tpu as pltpu
from jax.sharding import PartitionSpec as P

HALO = 2
BF = jnp.bfloat16
F32 = jnp.float32
VMEM = pl.BlockSpec(memory_space=pltpu.VMEM)


def peer(me, k, count):
    if count & (count - 1) == 0:
        return lax.bitwise_xor(me, jnp.int32(k))
    return lax.rem(me + k, jnp.int32(count))


def pairs_of(count, k):
    if count & (count - 1) == 0:
        return [(i, i ^ k) for i in range(count)]
    return [(i, (i + k) % count) for i in range(count)]


def to_peer(block, axis, k):
    return lax.ppermute(block, axis, pairs_of(lax.axis_size(axis), k))


def to_origin(block, axis, k):
    return lax.ppermute(block, axis, [(b, a) for a, b in pairs_of(lax.axis_size(axis), k)])


def call(body, out_shape, *args, scratch=(), flops=0, hbm=False, after=()):
    moved = sum(a.size * 4 for a in args)
    many = isinstance(out_shape, (tuple, list))
    if hbm:
        args = [pltpu.with_memory_space_constraint(a, pltpu.HBM) for a in args]
    space = pltpu.HBM if hbm else pltpu.VMEM
    count = len(args)

    def run(*refs):
        body(*refs[:count], *refs[count + len(after) :])

    return pl.pallas_call(
        run,
        out_shape=out_shape,
        in_specs=[pl.BlockSpec(memory_space=space)] * count
        + [pl.BlockSpec(memory_space=pl.ANY)] * len(after),
        out_specs=[VMEM] * len(out_shape) if many else VMEM,
        scratch_shapes=scratch,
        cost_estimate=pl.CostEstimate(flops=flops, bytes_accessed=moved, transcendentals=0),
        compiler_params=pltpu.CompilerParams(vmem_limit_bytes=24 << 20),
    )(*args, *after)


def pack_kernel(views, share, feat_hbm, row_hbm, col_hbm, frac_hbm, *refs):
    outs = refs[:views]
    feat_ref, row_ref, col_ref, frac_ref, sems = refs[views:]
    copies = [
        pltpu.make_async_copy(source, target, sems.at[i])
        for i, (source, target) in enumerate(
            ((feat_hbm, feat_ref), (row_hbm, row_ref), (col_hbm, col_ref), (frac_hbm, frac_ref))
        )
    ]
    for copy in copies:
        copy.start()
    for copy in copies:
        copy.wait()
    me = lax.axis_index("view")
    planes, rows = row_ref.shape[1:3]
    first = lax.axis_index("row") * rows
    width = feat_ref.shape[3]
    lanes = outs[0].shape[1]
    pages = -(-planes * rows // lanes)
    for d in range(planes):
        for y in range(rows):
            page, line = divmod(d * rows + y, lanes)
            top = (row_ref[0, d, y : y + 1, :] - (first + y - HALO)).astype(F32)
            col = col_ref[0, d, y : y + 1, :].astype(F32)
            fy = frac_ref[0, 0, d, y : y + 1, :].astype(F32) / 256.0
            fx = frac_ref[1, 0, d, y : y + 1, :].astype(F32) / 256.0
            for kind, value in enumerate((top, col, fy, fx)):
                for k in range(views):
                    outs[k][rows + kind * pages + page, line : line + 1, :] = value
    for k in range(views):
        base = peer(me, k, views) * share
        for y in range(rows):
            if share % 8:
                outs[k][y] = jnp.zeros((lanes, width), F32)
            for c in range(share):
                outs[k][y, c : c + 1, :] = feat_ref[0, base + c, y : y + 1, :]


def split(x):
    high = x.astype(BF)
    return high, (x - high.astype(F32)).astype(BF)


class Sizes:
    def __init__(self, packet, planes, rows):
        self.planes, self.rows = planes, rows
        self.lanes, self.width = packet.shape[1:]
        self.pages = -(-planes * rows // self.lanes)
        self.block = 256 if self.width % 256 == 0 else self.width
        self.segments = self.width // self.block
        self.window = 2 * HALO + 1
        self.padded = rows + 2 * HALO
        self.tall = self.segments * self.window * 2 * self.lanes

    def lookups(self):
        return pltpu.VMEM((self.window + 4 + self.segments, self.pages * self.lanes, self.width), F32)

    def one_hot(self, turned=False):
        length = self.planes * self.width
        return (self.rows,) + ((length, self.block) if turned else (self.block, length))


def look_up(z, packet, t_ref):
    for page in range(z.pages):
        top, col, fy, fx = (packet[z.rows + kind * z.pages + page] for kind in range(4))
        lines = slice(page * z.lanes, (page + 1) * z.lanes)
        for i in range(z.window):
            t_ref[i, lines] = jnp.where(top == i, 1.0 - fy, jnp.where(top == i - 1, fy, 0.0))
        segment = jnp.zeros_like(col)
        for j in range(1, z.segments):
            segment = segment + jnp.where(col >= float(j * z.block), 1.0, 0.0)
        local = col - segment * float(z.block)
        t_ref[z.window, lines] = local
        t_ref[z.window + 1, lines] = segment
        t_ref[z.window + 2, lines] = 1.0 - fx
        t_ref[z.window + 3, lines] = fx
        for j in range(1, z.segments):
            border = (local == float(z.block - 1)) & (segment == float(j - 1))
            t_ref[z.window + 3 + j, lines] = jnp.where(border, fx, 0.0)


def build(z, t_ref, w_ref, d, y):
    at = pl.ds(d * z.rows + y, 1)
    local = t_ref[z.window, at, :]
    here, after = local.astype(BF), (local + 1.0).astype(BF)
    left, right = t_ref[z.window + 2, at, :].astype(BF), t_ref[z.window + 3, at, :].astype(BF)
    it = lax.broadcasted_iota(jnp.int32, (z.block, z.width), 0).astype(F32).astype(BF)
    hot = jnp.where(it == here, left, jnp.where(it == after, right, jnp.zeros((), BF)))
    columns = pl.ds(pl.multiple_of(d * z.width, 128), z.width)
    w_ref[y, :, columns] = hot


def each_plane(z, unroll, step):
    if unroll:
        for d in range(z.planes):
            step(d)
    else:
        lax.fori_loop(0, z.planes, lambda d, carry: (step(d), carry)[1], 0)


def forward(z, unroll, fresh, packet, halo, warped_ref, w_ref, t_ref, f_ref, b_ref):
    is_first = lax.axis_index("row") == 0
    look_up(z, packet, t_ref)
    half = z.window * 2 * z.lanes
    for r in range(z.padded):
        if r < HALO:
            x = jnp.where(is_first, 0.0, halo[z.rows - HALO + r])
        elif r < HALO + z.rows:
            x = packet[r - HALO]
        else:
            x = jnp.where(is_first, halo[r - HALO - z.rows], 0.0)
        both = jnp.concatenate(split(x), axis=0)
        for j in range(z.segments):
            for y in range(z.rows):
                if 0 <= r - y < z.window:
                    at = j * half + (r - y) * 2 * z.lanes
                    f_ref[y, at : at + 2 * z.lanes] = both[:, j * z.block : (j + 1) * z.block]
            if j:
                b_ref[r, j - 1] = jnp.broadcast_to(x[:, j * z.block : j * z.block + 1], x.shape)

    def step(d):
        for y in range(z.rows):
            if fresh:
                build(z, t_ref, w_ref, d, y)
            at = pl.ds(d * z.rows + y, 1)
            columns = pl.ds(pl.multiple_of(d * z.width, 128), z.width)
            p = jnp.dot(f_ref[y], w_ref[y, :, columns], preferred_element_type=F32)
            segment = t_ref[z.window + 1, at, :]
            total = 0.0
            for i in range(z.window):
                value = 0.0
                for j in range(z.segments):
                    low = j * half + i * 2 * z.lanes
                    part = p[low : low + z.lanes] + p[low + z.lanes : low + 2 * z.lanes]
                    value = jnp.where(segment == float(j), part, value)
                for j in range(1, z.segments):
                    value = value + t_ref[z.window + 3 + j, at, :] * b_ref[y + i, j - 1]
                total = total + t_ref[i, at, :] * value
            warped_ref[d, y] = total

    each_plane(z, unroll, step)


def hot_kernel(z, unroll, packet, hot, t_ref):
    look_up(z, packet, t_ref)

    def step(d):
        for y in range(z.rows):
            build(z, t_ref, hot, d, y)

    each_plane(z, unroll, step)


def ahead_kernel(z, unroll, keep, turned, count, *refs):
    packets, halo, refs = refs[:count], refs[count], refs[count + 1 :]
    if keep:
        hots, refs = refs[:count], refs[count:]
    t_ref, f_ref, b_ref = refs[-3:]
    for v in range(count):
        hot = hots[v] if keep else refs[-4]
        forward(z, unroll, not keep, packets[v], halo.at[v], refs[v], hot, t_ref, f_ref, b_ref)
        if turned:
            for y in range(z.rows):
                refs[count + v][y] = hot[y].T


def backward(z, unroll, share, views, packet, warped, mean_ref, cot_ref, hot, fresh, turned, work, own_ref, rim_ref):
    t_ref, l_ref, grad_ref, e_ref = work
    is_first = lax.axis_index("row") == 0
    half = z.window * 2 * z.lanes
    look_up(z, packet, t_ref)
    e_ref[...] = jnp.zeros_like(e_ref)

    def step(d):
        for y in range(z.rows):
            if fresh:
                build(z, t_ref, hot, d, y)
            at = pl.ds(d * z.rows + y, 1)
            columns = pl.ds(pl.multiple_of(d * z.width, 128), z.width)
            cot = cot_ref[d, :, y, :]
            if share % 8:
                rows = lax.broadcasted_iota(jnp.int32, (z.lanes, z.width), 0)
                wide = jnp.zeros((z.lanes, z.width), F32)
                for c in range(share):
                    wide = jnp.where(rows == c, cot[c : c + 1], wide)
                cot = wide
            g = (2.0 / views) * cot * (warped[d, y] - mean_ref[d, y])
            parts = []
            for i in range(z.window):
                term = t_ref[i, at, :] * g
                parts += split(term)
                for j in range(1, z.segments):
                    crossing = term * t_ref[z.window + 3 + j, at, :]
                    folded = crossing[:, :128]
                    for lane in range(128, z.width, 128):
                        folded = folded + crossing[:, lane : lane + 128]
                    e_ref[y + i, j - 1] += folded
            parts = jnp.concatenate(parts, axis=0)
            segment = t_ref[z.window + 1, at, :]
            for j in range(z.segments):
                mask = jnp.where(segment == float(j), 1.0, 0.0).astype(BF)
                l_ref[y, j * half : (j + 1) * half, columns] = parts * mask

    each_plane(z, unroll, step)
    for y in range(z.rows):
        p = lax.dot_general(
            l_ref[y], hot[y], (((1,), (0 if turned else 1,)), ((), ())), preferred_element_type=F32
        )
        for i in range(z.window):
            for j in range(z.segments):
                low = j * half + i * 2 * z.lanes
                part = p[low : low + z.lanes] + p[low + z.lanes : low + 2 * z.lanes]
                columns = slice(j * z.block, (j + 1) * z.block)
                if y and i < z.window - 1:
                    grad_ref[y + i, :, columns] += part
                else:
                    grad_ref[y + i, :, columns] = part
    for r in range(z.padded):
        for j in range(1, z.segments):
            extra = jnp.sum(e_ref[r, j - 1], axis=1, keepdims=True)
            lane = lax.broadcasted_iota(jnp.int32, (z.lanes, 128), 1)
            columns = slice(j * z.block, j * z.block + 128)
            grad_ref[r, :, columns] += jnp.where(lane == 0, extra, 0.0)
    for r in range(z.rows):
        own_ref[r] = grad_ref[HALO + r]
    for r in range(HALO):
        rim_ref[r] = jnp.where(is_first, grad_ref[HALO + z.rows + r], grad_ref[r])


def turn_kernel(z, unroll, keep, share, views, late, ids, *refs):
    count = len(ids)
    early, hots_in = views - late, (count if keep else 0)
    packets, refs = (refs[count - 1],) + refs[: count - 1], refs[count:]
    halo, cot_ref, refs = refs[0], refs[1], refs[2:]
    ahead, refs = refs[:early], refs[early:]
    hots, refs = refs[:hots_in], refs[hots_in:]
    own_ref, rim_ref, mean_ref, warped_ref, w_ref, t_ref, f_ref, b_ref, l_ref, grad_ref, e_ref = refs
    for v in range(late):
        hot = hots[count - late + v] if keep else w_ref.at[0]
        packet = packets[count - late + v]
        forward(z, unroll, not keep, packet, halo.at[v], warped_ref.at[v], hot, t_ref.at[0], f_ref, b_ref)
    warped = list(ahead) + [warped_ref.at[v] for v in range(late)]

    def average(d):
        for y in range(z.rows):
            mean_ref[d, y] = sum(w[d, y] for w in warped) / views

    each_plane(z, unroll, average)
    for v in reversed(range(count)):
        hot = w_ref.at[0]
        if keep:
            hot = hots[v]
        work = t_ref.at[v % 2], l_ref.at[v % 2], grad_ref.at[v % 2], e_ref.at[v % 2]
        backward(
            z, unroll, share, views, packets[v], warped[ids[v]], mean_ref, cot_ref, hot,
            not keep, keep and hot.shape != w_ref.at[0].shape, work, own_ref.at[v], rim_ref.at[v],
        )


def rest_kernel(z, unroll, keep, share, views, count, *refs):
    packets, cot_ref, mean_ref, refs = refs[:count], refs[count], refs[count + 1], refs[count + 2 :]
    warped, refs = refs[:count], refs[count:]
    if keep:
        hots, refs = refs[:count], refs[count:]
    own_ref, rim_ref = refs[:2]
    t_ref, l_ref, grad_ref, e_ref = refs[-4:]
    for v in reversed(range(count)):
        work = t_ref.at[v % 2], l_ref.at[v % 2], grad_ref.at[v % 2], e_ref.at[v % 2]
        backward(
            z, unroll, share, views, packets[v], warped[v], mean_ref, cot_ref,
            hots[v] if keep else refs[2].at[0], not keep, False, work, own_ref.at[v], rim_ref.at[v],
        )


def stack_kernel(count, *refs):
    for v in range(count):
        refs[count][v] = refs[v][...]


def copy_kernel(in_ref, out_ref):
    out_ref[...] = in_ref[...]


def rows_kernel(count, *refs):
    rows = refs[count].shape[1]
    for v in range(count):
        refs[count][v] = refs[v][:rows]


def fold_kernel(depths, own_ref, rim_ref, *outs):
    views, rows, lanes, width = own_ref.shape
    part = width // depths
    me = lax.axis_index("depth")
    for k in range(depths):
        at = pl.multiple_of(peer(me, k, depths) * part, part)
        for v in range(views):
            for r in range(rows):
                outs[k][v, r] = own_ref[v, r, :, pl.ds(at, part)]
    is_first = lax.axis_index("row") == 0
    for k in range(depths):
        at = pl.multiple_of(peer(me, k, depths) * part, part)
        for v in range(views):
            for r in range(HALO):
                upper, lower = r, rows - HALO + r
                value = rim_ref[v, r, :, pl.ds(at, part)]
                outs[k][v, upper] += jnp.where(is_first, 0.0, value)
                outs[k][v, lower] += jnp.where(is_first, value, 0.0)


def sum_kernel(depths, views, *refs):
    for v in range(views):
        total = refs[0][v]
        for k in range(1, depths):
            total = total + refs[k][v]
        refs[depths + v][...] = total


def place_kernel(views, share, *refs):
    near, out_ref = len(refs) - 2, refs[-1]
    me = lax.axis_index("view")
    rows = out_ref.shape[2]
    for k in range(views):
        piece = refs[k + 1] if k < near else refs[0].at[views - 1 - k]
        base = peer(me, k, views) * share
        for c in range(share):
            for r in range(rows):
                out_ref[0, base + c, r : r + 1, :] = piece[r, c : c + 1, :]


def per_device(features, cotangent, src_row, src_col, fractions):
    views = lax.axis_size("view")
    depths = lax.axis_size("depth")
    channels, rows, width = features.shape[1:]
    planes, share = cotangent.shape[:2]
    lanes = -(-share // 8) * 8
    pages = -(-planes * rows // lanes)
    packet = jax.ShapeDtypeStruct((rows + 4 * pages, lanes, width), F32)
    packets = call(
        functools.partial(pack_kernel, views, share),
        [packet] * views,
        features, src_row, src_col, fractions,
        scratch=[
            pltpu.VMEM(a.shape, a.dtype) for a in (features, src_row, src_col, fractions)
        ] + [pltpu.SemaphoreType.DMA((4,))],
        hbm=True,
    )
    packets = list(packets)
    z = Sizes(packet, planes, rows)
    keep = unroll = views <= 4
    if views <= 4:
        groups = [[k] for k in range(views)]
    else:
        groups = [[0], list(range(1, views // 2)), list(range(views // 2, views - 1)), [views - 1]]
    late = len(groups[-1])
    hot = jax.ShapeDtypeStruct(z.one_hot(), BF)
    warp = jax.ShapeDtypeStruct((planes, rows, lanes, width), F32)
    tables = [
        z.lookups(),
        pltpu.VMEM((rows, z.tall, z.block), BF),
        pltpu.VMEM((z.padded, max(z.segments - 1, 1), lanes, width), F32),
    ]
    flops = 2 * planes * rows * width * z.block * z.tall

    def halo_of(group, after=()):
        own_rows = call(
            functools.partial(rows_kernel, len(group)),
            jax.ShapeDtypeStruct((len(group), rows, lanes, width), F32),
            *[packets[k] for k in group],
            after=after,
        )
        return own_rows, to_peer(own_rows, "row", 1)

    def hot_of(k, after=()):
        return call(
            functools.partial(hot_kernel, z, unroll), hot, packets[k],
            scratch=[z.lookups()], flops=flops // 4, after=after,
        )

    def ahead(group, halo, hots, after=(), turned=False):
        count = len(group)
        shape = jax.ShapeDtypeStruct(z.one_hot(turned), BF)
        results = call(
            functools.partial(ahead_kernel, z, unroll, keep, turned, count),
            [warp] * count + ([shape] * count if turned else []),
            *[packets[k] for k in group], halo, *hots,
            scratch=([] if keep else [pltpu.VMEM(hot.shape, BF)]) + tables,
            flops=flops * count,
            after=after,
        )
        results = list(results)
        return results[:count], results[count:] or list(hots)

    own_halo = halo_of([0])[1]
    for k in range(1, views):
        packets[k] = to_peer(packets[k], "view", k)
    warped, hots = ahead([0], own_halo, [hot_of(0)] if keep else [], turned=keep)
    middle = list(range(1, views - late))
    sent, middle_halo = halo_of(middle[::-1], warped)
    raw = {k: [hot_of(k, (sent,))] if keep else [] for k in middle}
    last_sent, last_halo = halo_of(groups[-1], (sent, *sum(raw.values(), [])))
    for k in middle:
        at = len(middle) - k
        after = (last_sent,) if k == 1 else warped[-1:]
        more, more_hots = ahead([k], middle_halo[at : at + 1], raw[k], after)
        warped, hots = warped + more, hots + more_hots
    if keep:
        hots += [hot_of(k, (last_sent,)) for k in groups[-1]]
    first = max(views // 4, 1)
    near = list(range(1, first + 1))
    main = [0] + list(range(first + 1, views))
    last = len(main)
    work = [
        pltpu.VMEM((2, rows, z.tall, planes * width), BF),
        pltpu.VMEM((2, z.padded, lanes, width), F32),
        pltpu.VMEM((2, z.padded, max(z.segments - 1, 1), lanes, 128), F32),
    ]
    twice = pltpu.VMEM((2,) + z.lookups().shape, F32)

    def results_of(count):
        return [
            jax.ShapeDtypeStruct((count, rows, lanes, width), F32),
            jax.ShapeDtypeStruct((count, HALO, lanes, width), F32),
        ]

    own, rim, mean = call(
        functools.partial(turn_kernel, z, unroll, keep, share, views, late, tuple(main)),
        results_of(last) + [warp],
        *[packets[k] for k in main[1:]], packets[0], last_halo, cotangent, *warped,
        *([hots[k] for k in main] if keep else []),
        scratch=[
            pltpu.VMEM((late,) + warp.shape, F32),
            pltpu.VMEM((1,) + hot.shape, BF),
            twice, *tables[1:], *work,
        ],
        flops=flops * (last + late),
    )
    rim = call(copy_kernel, jax.ShapeDtypeStruct(rim.shape, F32), rim)
    own_rest, rim_rest = call(
        functools.partial(rest_kernel, z, unroll, keep, share, views, first),
        results_of(first),
        *[packets[k] for k in near], cotangent, mean, *[warped[k] for k in near],
        *([hots[k] for k in near] if keep else []),
        scratch=([] if keep else [pltpu.VMEM((1,) + hot.shape, BF)]) + [twice, *work],
        flops=flops * first,
        after=(rim,),
    )
    part = width // depths
    pieces = {}
    for ids, own, rim, after in ((main, own, rim, (own_rest,)), (near, own_rest, rim_rest, ())):
        count = own.shape[0]
        rim = to_peer(rim, "row", 1)
        halves = call(
            functools.partial(fold_kernel, depths),
            [jax.ShapeDtypeStruct((count, rows, lanes, part), F32)] * depths,
            own, rim,
            after=after,
        )
        halves = [halves[0]] + [to_peer(halves[k], "depth", k) for k in range(1, depths)]
        sums = call(
            functools.partial(sum_kernel, depths, count),
            [jax.ShapeDtypeStruct((rows, lanes, part), F32)] * count,
            *halves,
        )
        pieces.update(zip(ids, sums))
    back = [pieces[0]] + [to_origin(pieces[k], "view", k) for k in range(1, views)]
    edge = first + 1
    far = call(
        functools.partial(stack_kernel, views - edge),
        jax.ShapeDtypeStruct((views - edge, rows, lanes, part), F32),
        *back[:first:-1],
    )
    return call(
        functools.partial(place_kernel, views, share),
        jax.ShapeDtypeStruct((1, channels, rows, part), F32),
        far, *back[:edge],
    )


def solution(mesh):
    in_specs = (
        P("view", None, ("group", "row"), None),
        P("depth", "view", ("group", "row"), None),
        P("view", "depth", ("group", "row"), None),
        P("view", "depth", ("group", "row"), None),
        P(None, "view", "depth", ("group", "row"), None),
    )
    out_specs = P("view", None, ("group", "row"), "depth")
    return jax.shard_map(
        per_device, mesh=mesh, in_specs=in_specs, out_specs=out_specs, check_vma=False
    )
```

```python
import functools

import jax
import jax.numpy as jnp
from jax import lax
from jax.experimental import pallas as pl
from jax.experimental.pallas import tpu as pltpu
from jax.sharding import PartitionSpec as P

HALO = 2
BF = jnp.bfloat16
F32 = jnp.float32
VMEM = pl.BlockSpec(memory_space=pltpu.VMEM)


def peer(me, k, count):
    if count & (count - 1) == 0:
        return lax.bitwise_xor(me, jnp.int32(k))
    return lax.rem(me + k, jnp.int32(count))


def pairs_of(count, k):
    if count & (count - 1) == 0:
        return [(i, i ^ k) for i in range(count)]
    return [(i, (i + k) % count) for i in range(count)]


def to_peer(block, axis, k):
    return lax.ppermute(block, axis, pairs_of(lax.axis_size(axis), k))


def to_origin(block, axis, k):
    return lax.ppermute(block, axis, [(b, a) for a, b in pairs_of(lax.axis_size(axis), k)])


def call(body, out_shape, *args, scratch=(), flops=0, hbm=False, after=()):
    moved = sum(a.size * 4 for a in args)
    many = isinstance(out_shape, (tuple, list))
    if hbm:
        args = [pltpu.with_memory_space_constraint(a, pltpu.HBM) for a in args]
    space = pltpu.HBM if hbm else pltpu.VMEM
    count = len(args)

    def run(*refs):
        body(*refs[:count], *refs[count + len(after) :])

    return pl.pallas_call(
        run,
        out_shape=out_shape,
        in_specs=[pl.BlockSpec(memory_space=space)] * count
        + [pl.BlockSpec(memory_space=pl.ANY)] * len(after),
        out_specs=[VMEM] * len(out_shape) if many else VMEM,
        scratch_shapes=scratch,
        cost_estimate=pl.CostEstimate(flops=flops, bytes_accessed=moved, transcendentals=0),
        compiler_params=pltpu.CompilerParams(vmem_limit_bytes=24 << 20),
    )(*args, *after)


def pack_kernel(views, share, feat_hbm, row_hbm, col_hbm, frac_hbm, *refs):
    outs = refs[:views]
    feat_ref, row_ref, col_ref, frac_ref, sems = refs[views:]
    copies = [
        pltpu.make_async_copy(source, target, sems.at[i])
        for i, (source, target) in enumerate(
            ((feat_hbm, feat_ref), (row_hbm, row_ref), (col_hbm, col_ref), (frac_hbm, frac_ref))
        )
    ]
    for copy in copies:
        copy.start()
    for copy in copies:
        copy.wait()
    me = lax.axis_index("view")
    planes, rows = row_ref.shape[1:3]
    first = lax.axis_index("row") * rows
    width = feat_ref.shape[3]
    lanes = outs[0].shape[1]
    pages = -(-planes * rows // lanes)
    for d in range(planes):
        for y in range(rows):
            page, line = divmod(d * rows + y, lanes)
            top = (row_ref[0, d, y : y + 1, :] - (first + y - HALO)).astype(F32)
            col = col_ref[0, d, y : y + 1, :].astype(F32)
            fy = frac_ref[0, 0, d, y : y + 1, :].astype(F32) / 256.0
            fx = frac_ref[1, 0, d, y : y + 1, :].astype(F32) / 256.0
            for kind, value in enumerate((top, col, fy, fx)):
                for k in range(views):
                    outs[k][rows + kind * pages + page, line : line + 1, :] = value
    for k in range(views):
        base = peer(me, k, views) * share
        for y in range(rows):
            if share % 8:
                outs[k][y] = jnp.zeros((lanes, width), F32)
            for c in range(share):
                outs[k][y, c : c + 1, :] = feat_ref[0, base + c, y : y + 1, :]


def split(x):
    high = x.astype(BF)
    return high, (x - high.astype(F32)).astype(BF)


class Sizes:
    def __init__(self, packet, planes, rows):
        self.planes, self.rows = planes, rows
        self.lanes, self.width = packet.shape[1:]
        self.pages = -(-planes * rows // self.lanes)
        self.block = 256 if self.width % 256 == 0 else self.width
        self.segments = self.width // self.block
        self.window = 2 * HALO + 1
        self.padded = rows + 2 * HALO
        self.tall = self.segments * self.window * 2 * self.lanes

    def lookups(self):
        return pltpu.VMEM((self.window + 4 + self.segments, self.pages * self.lanes, self.width), F32)

    def one_hot(self, turned=False):
        length = self.planes * self.width
        return (self.rows,) + ((length, self.block) if turned else (self.block, length))


def look_up(z, packet, t_ref):
    for page in range(z.pages):
        top, col, fy, fx = (packet[z.rows + kind * z.pages + page] for kind in range(4))
        lines = slice(page * z.lanes, (page + 1) * z.lanes)
        for i in range(z.window):
            t_ref[i, lines] = jnp.where(top == i, 1.0 - fy, jnp.where(top == i - 1, fy, 0.0))
        segment = jnp.zeros_like(col)
        for j in range(1, z.segments):
            segment = segment + jnp.where(col >= float(j * z.block), 1.0, 0.0)
        local = col - segment * float(z.block)
        t_ref[z.window, lines] = local
        t_ref[z.window + 1, lines] = segment
        t_ref[z.window + 2, lines] = 1.0 - fx
        t_ref[z.window + 3, lines] = fx
        for j in range(1, z.segments):
            border = (local == float(z.block - 1)) & (segment == float(j - 1))
            t_ref[z.window + 3 + j, lines] = jnp.where(border, fx, 0.0)


def build(z, t_ref, w_ref, d, y):
    at = pl.ds(d * z.rows + y, 1)
    local = t_ref[z.window, at, :]
    here, after = local.astype(BF), (local + 1.0).astype(BF)
    left, right = t_ref[z.window + 2, at, :].astype(BF), t_ref[z.window + 3, at, :].astype(BF)
    it = lax.broadcasted_iota(jnp.int32, (z.block, z.width), 0).astype(F32).astype(BF)
    hot = jnp.where(it == here, left, jnp.where(it == after, right, jnp.zeros((), BF)))
    columns = pl.ds(pl.multiple_of(d * z.width, 128), z.width)
    w_ref[y, :, columns] = hot


def each_plane(z, unroll, step):
    if unroll:
        for d in range(z.planes):
            step(d)
    else:
        lax.fori_loop(0, z.planes, lambda d, carry: (step(d), carry)[1], 0)


def forward(z, unroll, fresh, packet, halo, warped_ref, w_ref, t_ref, f_ref, b_ref):
    is_first = lax.axis_index("row") == 0
    look_up(z, packet, t_ref)
    half = z.window * 2 * z.lanes
    for r in range(z.padded):
        if r < HALO:
            x = jnp.where(is_first, 0.0, halo[z.rows - HALO + r])
        elif r < HALO + z.rows:
            x = packet[r - HALO]
        else:
            x = jnp.where(is_first, halo[r - HALO - z.rows], 0.0)
        both = jnp.concatenate(split(x), axis=0)
        for j in range(z.segments):
            for y in range(z.rows):
                if 0 <= r - y < z.window:
                    at = j * half + (r - y) * 2 * z.lanes
                    f_ref[y, at : at + 2 * z.lanes] = both[:, j * z.block : (j + 1) * z.block]
            if j:
                b_ref[r, j - 1] = jnp.broadcast_to(x[:, j * z.block : j * z.block + 1], x.shape)

    def step(d):
        for y in range(z.rows):
            if fresh:
                build(z, t_ref, w_ref, d, y)
            at = pl.ds(d * z.rows + y, 1)
            columns = pl.ds(pl.multiple_of(d * z.width, 128), z.width)
            p = jnp.dot(f_ref[y], w_ref[y, :, columns], preferred_element_type=F32)
            segment = t_ref[z.window + 1, at, :]
            total = 0.0
            for i in range(z.window):
                value = 0.0
                for j in range(z.segments):
                    low = j * half + i * 2 * z.lanes
                    part = p[low : low + z.lanes] + p[low + z.lanes : low + 2 * z.lanes]
                    value = jnp.where(segment == float(j), part, value)
                for j in range(1, z.segments):
                    value = value + t_ref[z.window + 3 + j, at, :] * b_ref[y + i, j - 1]
                total = total + t_ref[i, at, :] * value
            warped_ref[d, y] = total

    each_plane(z, unroll, step)


def hot_kernel(z, unroll, packet, hot, t_ref):
    look_up(z, packet, t_ref)

    def step(d):
        for y in range(z.rows):
            build(z, t_ref, hot, d, y)

    each_plane(z, unroll, step)


def ahead_kernel(z, unroll, keep, turned, count, *refs):
    packets, halo, refs = refs[:count], refs[count], refs[count + 1 :]
    if keep:
        hots, refs = refs[:count], refs[count:]
    t_ref, f_ref, b_ref = refs[-3:]
    for v in range(count):
        hot = hots[v] if keep else refs[-4]
        forward(z, unroll, not keep, packets[v], halo.at[v], refs[v], hot, t_ref, f_ref, b_ref)
        if turned:
            for y in range(z.rows):
                refs[count + v][y] = hot[y].T


def backward(z, unroll, share, views, packet, warped, mean_ref, cot_ref, hot, fresh, turned, work, own_ref, rim_ref):
    t_ref, l_ref, grad_ref, e_ref = work
    is_first = lax.axis_index("row") == 0
    half = z.window * 2 * z.lanes
    look_up(z, packet, t_ref)
    e_ref[...] = jnp.zeros_like(e_ref)

    def step(d):
        for y in range(z.rows):
            if fresh:
                build(z, t_ref, hot, d, y)
            at = pl.ds(d * z.rows + y, 1)
            columns = pl.ds(pl.multiple_of(d * z.width, 128), z.width)
            cot = cot_ref[d, :, y, :]
            if share % 8:
                rows = lax.broadcasted_iota(jnp.int32, (z.lanes, z.width), 0)
                wide = jnp.zeros((z.lanes, z.width), F32)
                for c in range(share):
                    wide = jnp.where(rows == c, cot[c : c + 1], wide)
                cot = wide
            g = (2.0 / views) * cot * (warped[d, y] - mean_ref[d, y])
            parts = []
            for i in range(z.window):
                term = t_ref[i, at, :] * g
                parts += split(term)
                for j in range(1, z.segments):
                    crossing = term * t_ref[z.window + 3 + j, at, :]
                    folded = crossing[:, :128]
                    for lane in range(128, z.width, 128):
                        folded = folded + crossing[:, lane : lane + 128]
                    e_ref[y + i, j - 1] += folded
            parts = jnp.concatenate(parts, axis=0)
            segment = t_ref[z.window + 1, at, :]
            for j in range(z.segments):
                mask = jnp.where(segment == float(j), 1.0, 0.0).astype(BF)
                l_ref[y, j * half : (j + 1) * half, columns] = parts * mask

    each_plane(z, unroll, step)
    for y in range(z.rows):
        p = lax.dot_general(
            l_ref[y], hot[y], (((1,), (0 if turned else 1,)), ((), ())), preferred_element_type=F32
        )
        for i in range(z.window):
            for j in range(z.segments):
                low = j * half + i * 2 * z.lanes
                part = p[low : low + z.lanes] + p[low + z.lanes : low + 2 * z.lanes]
                columns = slice(j * z.block, (j + 1) * z.block)
                if y and i < z.window - 1:
                    grad_ref[y + i, :, columns] += part
                else:
                    grad_ref[y + i, :, columns] = part
    for r in range(z.padded):
        for j in range(1, z.segments):
            extra = jnp.sum(e_ref[r, j - 1], axis=1, keepdims=True)
            lane = lax.broadcasted_iota(jnp.int32, (z.lanes, 128), 1)
            columns = slice(j * z.block, j * z.block + 128)
            grad_ref[r, :, columns] += jnp.where(lane == 0, extra, 0.0)
    for r in range(z.rows):
        own_ref[r] = grad_ref[HALO + r]
    for r in range(HALO):
        rim_ref[r] = jnp.where(is_first, grad_ref[HALO + z.rows + r], grad_ref[r])


def turn_kernel(z, unroll, keep, share, views, late, ids, *refs):
    count = len(ids)
    early, hots_in = views - late, (count if keep else 0)
    packets, refs = refs[:count], refs[count:]
    halo, cot_ref, refs = refs[0], refs[1], refs[2:]
    ahead, refs = refs[:early], refs[early:]
    hots, refs = refs[:hots_in], refs[hots_in:]
    own_ref, rim_ref, mean_ref, warped_ref, w_ref, t_ref, f_ref, b_ref, l_ref, grad_ref, e_ref = refs
    for v in range(late):
        hot = hots[count - late + v] if keep else w_ref.at[0]
        packet = packets[count - late + v]
        forward(z, unroll, not keep, packet, halo.at[v], warped_ref.at[v], hot, t_ref.at[0], f_ref, b_ref)
    warped = list(ahead) + [warped_ref.at[v] for v in range(late)]

    def average(d):
        for y in range(z.rows):
            mean_ref[d, y] = sum(w[d, y] for w in warped) / views

    each_plane(z, unroll, average)
    for v in reversed(range(count)):
        hot = w_ref.at[0]
        if keep:
            hot = hots[v]
        work = t_ref.at[v % 2], l_ref.at[v % 2], grad_ref.at[v % 2], e_ref.at[v % 2]
        backward(
            z, unroll, share, views, packets[v], warped[ids[v]], mean_ref, cot_ref, hot,
            not keep, keep and hot.shape != w_ref.at[0].shape, work, own_ref.at[v], rim_ref.at[v],
        )


def rest_kernel(z, unroll, keep, share, views, count, *refs):
    packets, cot_ref, mean_ref, refs = refs[:count], refs[count], refs[count + 1], refs[count + 2 :]
    warped, refs = refs[:count], refs[count:]
    if keep:
        hots, refs = refs[:count], refs[count:]
    own_ref, rim_ref = refs[:2]
    t_ref, l_ref, grad_ref, e_ref = refs[-4:]
    for v in reversed(range(count)):
        work = t_ref.at[v % 2], l_ref.at[v % 2], grad_ref.at[v % 2], e_ref.at[v % 2]
        hot = hots[v] if keep else refs[2].at[0]
        backward(
            z, unroll, share, views, packets[v], warped[v], mean_ref, cot_ref, hot, not keep,
            hot.shape != z.one_hot(), work, own_ref.at[v], rim_ref.at[v],
        )


def stack_kernel(count, *refs):
    for v in range(count):
        refs[count][v] = refs[v][...]


def copy_kernel(in_ref, out_ref):
    out_ref[...] = in_ref[...]


def rows_kernel(count, *refs):
    rows = refs[count].shape[1]
    for v in range(count):
        refs[count][v] = refs[v][:rows]


def fold_kernel(depths, own_ref, rim_ref, *outs):
    views, rows, lanes, width = own_ref.shape
    part = width // depths
    me = lax.axis_index("depth")
    for k in range(depths):
        at = pl.multiple_of(peer(me, k, depths) * part, part)
        for v in range(views):
            for r in range(rows):
                outs[k][v, r] = own_ref[v, r, :, pl.ds(at, part)]
    is_first = lax.axis_index("row") == 0
    for k in range(depths):
        at = pl.multiple_of(peer(me, k, depths) * part, part)
        for v in range(views):
            for r in range(HALO):
                upper, lower = r, rows - HALO + r
                value = rim_ref[v, r, :, pl.ds(at, part)]
                outs[k][v, upper] += jnp.where(is_first, 0.0, value)
                outs[k][v, lower] += jnp.where(is_first, value, 0.0)


def sum_kernel(depths, views, *refs):
    for v in range(views):
        total = refs[0][v]
        for k in range(1, depths):
            total = total + refs[k][v]
        refs[depths + v][...] = total


def place_kernel(views, share, *refs):
    near, out_ref = len(refs) - 2, refs[-1]
    me = lax.axis_index("view")
    rows = out_ref.shape[2]
    for k in range(views):
        piece = refs[k + 1] if k < near else refs[0].at[views - 1 - k]
        base = peer(me, k, views) * share
        for c in range(share):
            for r in range(rows):
                out_ref[0, base + c, r : r + 1, :] = piece[r, c : c + 1, :]


def per_device(features, cotangent, src_row, src_col, fractions):
    views = lax.axis_size("view")
    depths = lax.axis_size("depth")
    channels, rows, width = features.shape[1:]
    planes, share = cotangent.shape[:2]
    lanes = -(-share // 8) * 8
    pages = -(-planes * rows // lanes)
    packet = jax.ShapeDtypeStruct((rows + 4 * pages, lanes, width), F32)
    packets = call(
        functools.partial(pack_kernel, views, share),
        [packet] * views,
        features, src_row, src_col, fractions,
        scratch=[
            pltpu.VMEM(a.shape, a.dtype) for a in (features, src_row, src_col, fractions)
        ] + [pltpu.SemaphoreType.DMA((4,))],
        hbm=True,
    )
    packets = list(packets)
    z = Sizes(packet, planes, rows)
    keep = unroll = views <= 4
    if views <= 4:
        groups = [[k] for k in range(views)]
    else:
        groups = [[0], list(range(1, views // 2)), list(range(views // 2, views - 1)), [views - 1]]
    late = len(groups[-1])
    hot = jax.ShapeDtypeStruct(z.one_hot(), BF)
    warp = jax.ShapeDtypeStruct((planes, rows, lanes, width), F32)
    tables = [
        z.lookups(),
        pltpu.VMEM((rows, z.tall, z.block), BF),
        pltpu.VMEM((z.padded, max(z.segments - 1, 1), lanes, width), F32),
    ]
    flops = 2 * planes * rows * width * z.block * z.tall

    def halo_of(group, after=()):
        own_rows = call(
            functools.partial(rows_kernel, len(group)),
            jax.ShapeDtypeStruct((len(group), rows, lanes, width), F32),
            *[packets[k] for k in group],
            after=after,
        )
        return own_rows, to_peer(own_rows, "row", 1)

    def hot_of(k, after=()):
        return call(
            functools.partial(hot_kernel, z, unroll), hot, packets[k],
            scratch=[z.lookups()], flops=flops // 4, after=after,
        )

    def ahead(group, halo, hots, after=(), turned=False):
        count = len(group)
        shape = jax.ShapeDtypeStruct(z.one_hot(turned), BF)
        results = call(
            functools.partial(ahead_kernel, z, unroll, keep, turned, count),
            [warp] * count + ([shape] * count if turned else []),
            *[packets[k] for k in group], halo, *hots,
            scratch=([] if keep else [pltpu.VMEM(hot.shape, BF)]) + tables,
            flops=flops * count,
            after=after,
        )
        results = list(results)
        return results[:count], results[count:] or list(hots)

    own_halo = halo_of([0])[1]
    for k in range(1, views):
        packets[k] = to_peer(packets[k], "view", k)
    warped, hots = ahead([0], own_halo, [hot_of(0)] if keep else [], turned=keep)
    middle = list(range(1, views - late))
    sent, middle_halo = halo_of(middle[::-1], warped)
    raw = {k: [hot_of(k, (sent,))] if keep else [] for k in middle}
    last_sent, last_halo = halo_of(groups[-1], (sent, *sum(raw.values(), [])))
    for k in middle:
        at = len(middle) - k
        after = (last_sent,) if k == 1 else warped[-1:]
        more, more_hots = ahead([k], middle_halo[at : at + 1], raw[k], after)
        warped, hots = warped + more, hots + more_hots
    if keep:
        hots += [hot_of(k, (last_sent,)) for k in groups[-1]]
    first = max(views // 4, 1)
    near = list(range(first + 1))
    main = list(range(first + 1, views))
    last = len(main)
    work = [
        pltpu.VMEM((2, rows, z.tall, planes * width), BF),
        pltpu.VMEM((2, z.padded, lanes, width), F32),
        pltpu.VMEM((2, z.padded, max(z.segments - 1, 1), lanes, 128), F32),
    ]
    twice = pltpu.VMEM((2,) + z.lookups().shape, F32)

    def results_of(count):
        return [
            jax.ShapeDtypeStruct((count, rows, lanes, width), F32),
            jax.ShapeDtypeStruct((count, HALO, lanes, width), F32),
        ]

    own, rim, mean = call(
        functools.partial(turn_kernel, z, unroll, keep, share, views, late, tuple(main)),
        results_of(last) + [warp],
        *[packets[k] for k in main], last_halo, cotangent, *warped,
        *([hots[k] for k in main] if keep else []),
        scratch=[
            pltpu.VMEM((late,) + warp.shape, F32),
            pltpu.VMEM((1,) + hot.shape, BF),
            twice, *tables[1:], *work,
        ],
        flops=flops * (last + late),
    )
    rim = call(copy_kernel, jax.ShapeDtypeStruct(rim.shape, F32), rim)
    own_rest, rim_rest = call(
        functools.partial(rest_kernel, z, unroll, keep, share, views, len(near)),
        results_of(len(near)),
        *[packets[k] for k in near], cotangent, mean, *[warped[k] for k in near],
        *([hots[k] for k in near] if keep else []),
        scratch=([] if keep else [pltpu.VMEM((1,) + hot.shape, BF)]) + [twice, *work],
        flops=flops * len(near),
        after=(rim,),
    )
    part = width // depths
    pieces, folded = {}, ()
    for ids, own, rim, after in ((main, own, rim, (own_rest,)), (near, own_rest, rim_rest, ())):
        count = own.shape[0]
        if folded:
            rim = call(copy_kernel, jax.ShapeDtypeStruct(rim.shape, F32), rim, after=folded)
        rim = to_peer(rim, "row", 1)
        halves = call(
            functools.partial(fold_kernel, depths),
            [jax.ShapeDtypeStruct((count, rows, lanes, part), F32)] * depths,
            own, rim,
            after=after,
        )
        folded = (halves[0],)
        halves = [halves[0]] + [to_peer(halves[k], "depth", k) for k in range(1, depths)]
        sums = call(
            functools.partial(sum_kernel, depths, count),
            [jax.ShapeDtypeStruct((rows, lanes, part), F32)] * count,
            *halves,
        )
        pieces.update(zip(ids, sums))
    back = [pieces[0]] + [to_origin(pieces[k], "view", k) for k in range(1, views)]
    edge = first + 1
    far = call(
        functools.partial(stack_kernel, views - edge),
        jax.ShapeDtypeStruct((views - edge, rows, lanes, part), F32),
        *back[:first:-1],
    )
    return call(
        functools.partial(place_kernel, views, share),
        jax.ShapeDtypeStruct((1, channels, rows, part), F32),
        far, *back[:edge],
    )


def solution(mesh):
    in_specs = (
        P("view", None, ("group", "row"), None),
        P("depth", "view", ("group", "row"), None),
        P("view", "depth", ("group", "row"), None),
        P("view", "depth", ("group", "row"), None),
        P(None, "view", "depth", ("group", "row"), None),
    )
    out_specs = P("view", None, ("group", "row"), "depth")
    return jax.shard_map(
        per_device, mesh=mesh, in_specs=in_specs, out_specs=out_specs, check_vma=False
    )
```

```python
import functools

import jax
import jax.numpy as jnp
from jax import lax
from jax.experimental import pallas as pl
from jax.experimental.pallas import tpu as pltpu
from jax.sharding import PartitionSpec as P

HALO = 2
BF = jnp.bfloat16
F32 = jnp.float32
VMEM = pl.BlockSpec(memory_space=pltpu.VMEM)


def peer(me, k, count):
    if count & (count - 1) == 0:
        return lax.bitwise_xor(me, jnp.int32(k))
    return lax.rem(me + k, jnp.int32(count))


def pairs_of(count, k):
    if count & (count - 1) == 0:
        return [(i, i ^ k) for i in range(count)]
    return [(i, (i + k) % count) for i in range(count)]


def to_peer(block, axis, k):
    return lax.ppermute(block, axis, pairs_of(lax.axis_size(axis), k))


def to_origin(block, axis, k):
    return lax.ppermute(block, axis, [(b, a) for a, b in pairs_of(lax.axis_size(axis), k)])


def call(body, out_shape, *args, scratch=(), flops=0, hbm=False, after=()):
    moved = sum(a.size * 4 for a in args)
    many = isinstance(out_shape, (tuple, list))
    if hbm:
        args = [pltpu.with_memory_space_constraint(a, pltpu.HBM) for a in args]
    space = pltpu.HBM if hbm else pltpu.VMEM
    count = len(args)

    def run(*refs):
        body(*refs[:count], *refs[count + len(after) :])

    return pl.pallas_call(
        run,
        out_shape=out_shape,
        in_specs=[pl.BlockSpec(memory_space=space)] * count
        + [pl.BlockSpec(memory_space=pl.ANY)] * len(after),
        out_specs=[VMEM] * len(out_shape) if many else VMEM,
        scratch_shapes=scratch,
        cost_estimate=pl.CostEstimate(flops=flops, bytes_accessed=moved, transcendentals=0),
        compiler_params=pltpu.CompilerParams(vmem_limit_bytes=24 << 20),
    )(*args, *after)


def pack_kernel(views, share, feat_hbm, row_hbm, col_hbm, frac_hbm, *refs):
    outs = refs[:views]
    feat_ref, row_ref, col_ref, frac_ref, sems = refs[views:]
    copies = [
        pltpu.make_async_copy(source, target, sems.at[i])
        for i, (source, target) in enumerate(
            ((feat_hbm, feat_ref), (row_hbm, row_ref), (col_hbm, col_ref), (frac_hbm, frac_ref))
        )
    ]
    for copy in copies:
        copy.start()
    for copy in copies:
        copy.wait()
    me = lax.axis_index("view")
    planes, rows = row_ref.shape[1:3]
    first = lax.axis_index("row") * rows
    width = feat_ref.shape[3]
    lanes = outs[0].shape[1]
    pages = -(-planes * rows // lanes)
    for d in range(planes):
        for y in range(rows):
            page, line = divmod(d * rows + y, lanes)
            top = (row_ref[0, d, y : y + 1, :] - (first + y - HALO)).astype(F32)
            col = col_ref[0, d, y : y + 1, :].astype(F32)
            fy = frac_ref[0, 0, d, y : y + 1, :].astype(F32) / 256.0
            fx = frac_ref[1, 0, d, y : y + 1, :].astype(F32) / 256.0
            for kind, value in enumerate((top, col, fy, fx)):
                for k in range(views):
                    outs[k][rows + kind * pages + page, line : line + 1, :] = value
    for k in range(views):
        base = peer(me, k, views) * share
        for y in range(rows):
            if share % 8:
                outs[k][y] = jnp.zeros((lanes, width), F32)
            for c in range(share):
                outs[k][y, c : c + 1, :] = feat_ref[0, base + c, y : y + 1, :]


def split(x):
    high = x.astype(BF)
    return high, (x - high.astype(F32)).astype(BF)


class Sizes:
    def __init__(self, packet, planes, rows):
        self.planes, self.rows = planes, rows
        self.lanes, self.width = packet.shape[1:]
        self.pages = -(-planes * rows // self.lanes)
        self.block = 256 if self.width % 256 == 0 else self.width
        self.segments = self.width // self.block
        self.window = 2 * HALO + 1
        self.padded = rows + 2 * HALO
        self.tall = self.segments * self.window * 2 * self.lanes

    def lookups(self):
        return pltpu.VMEM((self.window + 4 + self.segments, self.pages * self.lanes, self.width), F32)

    def one_hot(self, turned=False):
        length = self.planes * self.width
        return (self.rows,) + ((length, self.block) if turned else (self.block, length))


def look_up(z, packet, t_ref):
    for page in range(z.pages):
        top, col, fy, fx = (packet[z.rows + kind * z.pages + page] for kind in range(4))
        lines = slice(page * z.lanes, (page + 1) * z.lanes)
        for i in range(z.window):
            t_ref[i, lines] = jnp.where(top == i, 1.0 - fy, jnp.where(top == i - 1, fy, 0.0))
        segment = jnp.zeros_like(col)
        for j in range(1, z.segments):
            segment = segment + jnp.where(col >= float(j * z.block), 1.0, 0.0)
        local = col - segment * float(z.block)
        t_ref[z.window, lines] = local
        t_ref[z.window + 1, lines] = segment
        t_ref[z.window + 2, lines] = 1.0 - fx
        t_ref[z.window + 3, lines] = fx
        for j in range(1, z.segments):
            border = (local == float(z.block - 1)) & (segment == float(j - 1))
            t_ref[z.window + 3 + j, lines] = jnp.where(border, fx, 0.0)


def build(z, t_ref, w_ref, d, y):
    at = pl.ds(d * z.rows + y, 1)
    local = t_ref[z.window, at, :]
    here, after = local.astype(BF), (local + 1.0).astype(BF)
    left, right = t_ref[z.window + 2, at, :].astype(BF), t_ref[z.window + 3, at, :].astype(BF)
    it = lax.broadcasted_iota(jnp.int32, (z.block, z.width), 0).astype(F32).astype(BF)
    hot = jnp.where(it == here, left, jnp.where(it == after, right, jnp.zeros((), BF)))
    columns = pl.ds(pl.multiple_of(d * z.width, 128), z.width)
    w_ref[y, :, columns] = hot


def each_plane(z, unroll, step):
    if unroll:
        for d in range(z.planes):
            step(d)
    else:
        lax.fori_loop(0, z.planes, lambda d, carry: (step(d), carry)[1], 0)


def forward(z, unroll, fresh, packet, halo, warped_ref, w_ref, t_ref, f_ref, b_ref):
    is_first = lax.axis_index("row") == 0
    look_up(z, packet, t_ref)
    half = z.window * 2 * z.lanes
    for r in range(z.padded):
        if r < HALO:
            x = jnp.where(is_first, 0.0, halo[z.rows - HALO + r])
        elif r < HALO + z.rows:
            x = packet[r - HALO]
        else:
            x = jnp.where(is_first, halo[r - HALO - z.rows], 0.0)
        both = jnp.concatenate(split(x), axis=0)
        for j in range(z.segments):
            for y in range(z.rows):
                if 0 <= r - y < z.window:
                    at = j * half + (r - y) * 2 * z.lanes
                    f_ref[y, at : at + 2 * z.lanes] = both[:, j * z.block : (j + 1) * z.block]
            if j:
                b_ref[r, j - 1] = jnp.broadcast_to(x[:, j * z.block : j * z.block + 1], x.shape)

    def step(d):
        for y in range(z.rows):
            if fresh:
                build(z, t_ref, w_ref, d, y)
            at = pl.ds(d * z.rows + y, 1)
            columns = pl.ds(pl.multiple_of(d * z.width, 128), z.width)
            p = jnp.dot(f_ref[y], w_ref[y, :, columns], preferred_element_type=F32)
            segment = t_ref[z.window + 1, at, :]
            total = 0.0
            for i in range(z.window):
                value = 0.0
                for j in range(z.segments):
                    low = j * half + i * 2 * z.lanes
                    part = p[low : low + z.lanes] + p[low + z.lanes : low + 2 * z.lanes]
                    value = jnp.where(segment == float(j), part, value)
                for j in range(1, z.segments):
                    value = value + t_ref[z.window + 3 + j, at, :] * b_ref[y + i, j - 1]
                total = total + t_ref[i, at, :] * value
            warped_ref[d, y] = total

    each_plane(z, unroll, step)


def hot_kernel(z, unroll, packet, hot, t_ref):
    look_up(z, packet, t_ref)

    def step(d):
        for y in range(z.rows):
            build(z, t_ref, hot, d, y)

    each_plane(z, unroll, step)


def ahead_kernel(z, unroll, keep, turned, count, *refs):
    packets, halo, refs = refs[:count], refs[count], refs[count + 1 :]
    if keep:
        hots, refs = refs[:count], refs[count:]
    t_ref, f_ref, b_ref = refs[-3:]
    for v in range(count):
        hot = hots[v] if keep else refs[-4]
        forward(z, unroll, not keep, packets[v], halo.at[v], refs[v], hot, t_ref, f_ref, b_ref)
        if turned:
            for y in range(z.rows):
                refs[count + v][y] = hot[y].T


def backward(z, unroll, share, views, packet, warped, mean_ref, cot_ref, hot, fresh, turned, work, own_ref, rim_ref):
    t_ref, l_ref, grad_ref, e_ref = work
    is_first = lax.axis_index("row") == 0
    half = z.window * 2 * z.lanes
    look_up(z, packet, t_ref)
    e_ref[...] = jnp.zeros_like(e_ref)

    def step(d):
        for y in range(z.rows):
            if fresh:
                build(z, t_ref, hot, d, y)
            at = pl.ds(d * z.rows + y, 1)
            columns = pl.ds(pl.multiple_of(d * z.width, 128), z.width)
            cot = cot_ref[d, :, y, :]
            if share % 8:
                rows = lax.broadcasted_iota(jnp.int32, (z.lanes, z.width), 0)
                wide = jnp.zeros((z.lanes, z.width), F32)
                for c in range(share):
                    wide = jnp.where(rows == c, cot[c : c + 1], wide)
                cot = wide
            g = (2.0 / views) * cot * (warped[d, y] - mean_ref[d, y])
            parts = []
            for i in range(z.window):
                term = t_ref[i, at, :] * g
                parts += split(term)
                for j in range(1, z.segments):
                    crossing = term * t_ref[z.window + 3 + j, at, :]
                    folded = crossing[:, :128]
                    for lane in range(128, z.width, 128):
                        folded = folded + crossing[:, lane : lane + 128]
                    e_ref[y + i, j - 1] += folded
            parts = jnp.concatenate(parts, axis=0)
            segment = t_ref[z.window + 1, at, :]
            for j in range(z.segments):
                mask = jnp.where(segment == float(j), 1.0, 0.0).astype(BF)
                l_ref[y, j * half : (j + 1) * half, columns] = parts * mask

    each_plane(z, unroll, step)
    for y in range(z.rows):
        p = lax.dot_general(
            l_ref[y], hot[y], (((1,), (0 if turned else 1,)), ((), ())), preferred_element_type=F32
        )
        for i in range(z.window):
            for j in range(z.segments):
                low = j * half + i * 2 * z.lanes
                part = p[low : low + z.lanes] + p[low + z.lanes : low + 2 * z.lanes]
                columns = slice(j * z.block, (j + 1) * z.block)
                if y and i < z.window - 1:
                    grad_ref[y + i, :, columns] += part
                else:
                    grad_ref[y + i, :, columns] = part
    for r in range(z.padded):
        for j in range(1, z.segments):
            extra = jnp.sum(e_ref[r, j - 1], axis=1, keepdims=True)
            lane = lax.broadcasted_iota(jnp.int32, (z.lanes, 128), 1)
            columns = slice(j * z.block, j * z.block + 128)
            grad_ref[r, :, columns] += jnp.where(lane == 0, extra, 0.0)
    for r in range(z.rows):
        own_ref[r] = grad_ref[HALO + r]
    for r in range(HALO):
        rim_ref[r] = jnp.where(is_first, grad_ref[HALO + z.rows + r], grad_ref[r])


def turn_kernel(z, unroll, keep, share, views, late, ids, *refs):
    count = len(ids)
    early, hots_in = views - late, (count if keep else 0)
    packets, refs = refs[:count], refs[count:]
    halo, cot_ref, refs = refs[0], refs[1], refs[2:]
    ahead, refs = refs[:early], refs[early:]
    hots, refs = refs[:hots_in], refs[hots_in:]
    own_ref, rim_ref, mean_ref, warped_ref, w_ref, t_ref, f_ref, b_ref, l_ref, grad_ref, e_ref = refs
    for v in range(late):
        hot = hots[count - late + v] if keep else w_ref.at[0]
        packet = packets[count - late + v]
        forward(z, unroll, not keep, packet, halo.at[v], warped_ref.at[v], hot, t_ref.at[0], f_ref, b_ref)
    warped = list(ahead) + [warped_ref.at[v] for v in range(late)]

    def average(d):
        for y in range(z.rows):
            mean_ref[d, y] = sum(w[d, y] for w in warped) / views

    each_plane(z, unroll, average)
    for v in reversed(range(count)):
        hot = w_ref.at[0]
        if keep:
            hot = hots[v]
        work = t_ref.at[v % 2], l_ref.at[v % 2], grad_ref.at[v % 2], e_ref.at[v % 2]
        backward(
            z, unroll, share, views, packets[v], warped[ids[v]], mean_ref, cot_ref, hot,
            not keep, keep and hot.shape != w_ref.at[0].shape, work, own_ref.at[v], rim_ref.at[v],
        )


def rest_kernel(z, unroll, keep, share, views, count, *refs):
    packets, cot_ref, mean_ref, refs = refs[:count], refs[count], refs[count + 1], refs[count + 2 :]
    warped, refs = refs[:count], refs[count:]
    if keep:
        hots, refs = refs[:count], refs[count:]
    own_ref, rim_ref = refs[:2]
    t_ref, l_ref, grad_ref, e_ref = refs[-4:]
    for v in reversed(range(count)):
        work = t_ref.at[v % 2], l_ref.at[v % 2], grad_ref.at[v % 2], e_ref.at[v % 2]
        hot = hots[v] if keep else refs[2].at[0]
        backward(
            z, unroll, share, views, packets[v], warped[v], mean_ref, cot_ref, hot, not keep,
            hot.shape != z.one_hot(), work, own_ref.at[v], rim_ref.at[v],
        )


def stack_kernel(count, *refs):
    for v in range(count):
        refs[count][v] = refs[v][...]


def copy_kernel(in_ref, out_ref):
    out_ref[...] = in_ref[...]


def rows_kernel(count, *refs):
    rows = refs[count].shape[1]
    for v in range(count):
        refs[count][v] = refs[v][:rows]


def fold_kernel(depths, own_ref, rim_ref, *outs):
    views, rows, lanes, width = own_ref.shape
    part = width // depths
    me = lax.axis_index("depth")
    for k in range(depths):
        at = pl.multiple_of(peer(me, k, depths) * part, part)
        for v in range(views):
            for r in range(rows):
                outs[k][v, r] = own_ref[v, r, :, pl.ds(at, part)]
    is_first = lax.axis_index("row") == 0
    for k in range(depths):
        at = pl.multiple_of(peer(me, k, depths) * part, part)
        for v in range(views):
            for r in range(HALO):
                upper, lower = r, rows - HALO + r
                value = rim_ref[v, r, :, pl.ds(at, part)]
                outs[k][v, upper] += jnp.where(is_first, 0.0, value)
                outs[k][v, lower] += jnp.where(is_first, value, 0.0)


def sum_kernel(depths, views, *refs):
    for v in range(views):
        total = refs[0][v]
        for k in range(1, depths):
            total = total + refs[k][v]
        refs[depths + v][...] = total


def place_kernel(views, share, *refs):
    near, out_ref = len(refs) - 2, refs[-1]
    me = lax.axis_index("view")
    rows = out_ref.shape[2]
    for k in range(views):
        piece = refs[k + 1] if k < near else refs[0].at[views - 1 - k]
        base = peer(me, k, views) * share
        for c in range(share):
            for r in range(rows):
                out_ref[0, base + c, r : r + 1, :] = piece[r, c : c + 1, :]


def per_device(features, cotangent, src_row, src_col, fractions):
    views = lax.axis_size("view")
    depths = lax.axis_size("depth")
    channels, rows, width = features.shape[1:]
    planes, share = cotangent.shape[:2]
    lanes = -(-share // 8) * 8
    pages = -(-planes * rows // lanes)
    packet = jax.ShapeDtypeStruct((rows + 4 * pages, lanes, width), F32)
    packets = call(
        functools.partial(pack_kernel, views, share),
        [packet] * views,
        features, src_row, src_col, fractions,
        scratch=[
            pltpu.VMEM(a.shape, a.dtype) for a in (features, src_row, src_col, fractions)
        ] + [pltpu.SemaphoreType.DMA((4,))],
        hbm=True,
    )
    packets = list(packets)
    z = Sizes(packet, planes, rows)
    keep = unroll = views <= 4
    if views <= 4:
        groups = [[k] for k in range(views)]
    else:
        groups = [[0], list(range(1, views // 2)), list(range(views // 2, views - 1)), [views - 1]]
    late = len(groups[-1])
    hot = jax.ShapeDtypeStruct(z.one_hot(), BF)
    warp = jax.ShapeDtypeStruct((planes, rows, lanes, width), F32)
    tables = [
        z.lookups(),
        pltpu.VMEM((rows, z.tall, z.block), BF),
        pltpu.VMEM((z.padded, max(z.segments - 1, 1), lanes, width), F32),
    ]
    flops = 2 * planes * rows * width * z.block * z.tall

    def halo_of(group, after=()):
        own_rows = call(
            functools.partial(rows_kernel, len(group)),
            jax.ShapeDtypeStruct((len(group), rows, lanes, width), F32),
            *[packets[k] for k in group],
            after=after,
        )
        return own_rows, to_peer(own_rows, "row", 1)

    def hot_of(k, after=()):
        return call(
            functools.partial(hot_kernel, z, unroll), hot, packets[k],
            scratch=[z.lookups()], flops=flops // 4, after=after,
        )

    def ahead(group, halo, hots, after=(), turned=False):
        count = len(group)
        shape = jax.ShapeDtypeStruct(z.one_hot(turned), BF)
        results = call(
            functools.partial(ahead_kernel, z, unroll, keep, turned, count),
            [warp] * count + ([shape] * count if turned else []),
            *[packets[k] for k in group], halo, *hots,
            scratch=([] if keep else [pltpu.VMEM(hot.shape, BF)]) + tables,
            flops=flops * count,
            after=after,
        )
        results = list(results)
        return results[:count], results[count:] or list(hots)

    own_halo = halo_of([0])[1]
    for k in range(1, views):
        packets[k] = to_peer(packets[k], "view", k)
    warped, hots = ahead([0], own_halo, [hot_of(0)] if keep else [], turned=keep)
    middle = list(range(1, views - late))
    sent, middle_halo = halo_of(middle[::-1], warped)
    raw = {k: [hot_of(k, (sent,))] if keep else [] for k in middle}
    last_sent, last_halo = halo_of(groups[-1], (sent, *sum(raw.values(), [])))
    if keep and middle:
        back = middle[::-1]
        more, more_hots = ahead(back, middle_halo, sum([raw[k] for k in back], []), (last_sent,))
        warped, hots = warped + more[::-1], hots + more_hots[::-1]
    for k in [] if keep else middle:
        at = len(middle) - k
        after = (last_sent,) if k == 1 else warped[-1:]
        more, more_hots = ahead([k], middle_halo[at : at + 1], raw[k], after)
        warped, hots = warped + more, hots + more_hots
    if keep:
        hots += [hot_of(k, (last_sent,)) for k in groups[-1]]
    first = max(views // 4, 1)
    near = list(range(first + 1))
    main = list(range(first + 1, views))
    last = len(main)
    work = [
        pltpu.VMEM((2, rows, z.tall, planes * width), BF),
        pltpu.VMEM((2, z.padded, lanes, width), F32),
        pltpu.VMEM((2, z.padded, max(z.segments - 1, 1), lanes, 128), F32),
    ]
    twice = pltpu.VMEM((2,) + z.lookups().shape, F32)

    def results_of(count):
        return [
            jax.ShapeDtypeStruct((count, rows, lanes, width), F32),
            jax.ShapeDtypeStruct((count, HALO, lanes, width), F32),
        ]

    own, rim, mean = call(
        functools.partial(turn_kernel, z, unroll, keep, share, views, late, tuple(main)),
        results_of(last) + [warp],
        *[packets[k] for k in main], last_halo, cotangent, *warped,
        *([hots[k] for k in main] if keep else []),
        scratch=[
            pltpu.VMEM((late,) + warp.shape, F32),
            pltpu.VMEM((1,) + hot.shape, BF),
            twice, *tables[1:], *work,
        ],
        flops=flops * (last + late),
    )
    rim = call(copy_kernel, jax.ShapeDtypeStruct(rim.shape, F32), rim)
    own_rest, rim_rest = call(
        functools.partial(rest_kernel, z, unroll, keep, share, views, len(near)),
        results_of(len(near)),
        *[packets[k] for k in near], cotangent, mean, *[warped[k] for k in near],
        *([hots[k] for k in near] if keep else []),
        scratch=([] if keep else [pltpu.VMEM((1,) + hot.shape, BF)]) + [twice, *work],
        flops=flops * len(near),
        after=(rim,),
    )
    part = width // depths
    pieces, folded = {}, ()
    for ids, own, rim, after in ((main, own, rim, (own_rest,)), (near, own_rest, rim_rest, ())):
        count = own.shape[0]
        if folded:
            rim = call(copy_kernel, jax.ShapeDtypeStruct(rim.shape, F32), rim, after=folded)
        rim = to_peer(rim, "row", 1)
        halves = call(
            functools.partial(fold_kernel, depths),
            [jax.ShapeDtypeStruct((count, rows, lanes, part), F32)] * depths,
            own, rim,
            after=after,
        )
        folded = (halves[0],)
        halves = [halves[0]] + [to_peer(halves[k], "depth", k) for k in range(1, depths)]
        sums = call(
            functools.partial(sum_kernel, depths, count),
            [jax.ShapeDtypeStruct((rows, lanes, part), F32)] * count,
            *halves,
        )
        pieces.update(zip(ids, sums))
    back = [pieces[0]] + [to_origin(pieces[k], "view", k) for k in range(1, views)]
    edge = first + 1
    far = call(
        functools.partial(stack_kernel, views - edge),
        jax.ShapeDtypeStruct((views - edge, rows, lanes, part), F32),
        *back[:first:-1],
    )
    return call(
        functools.partial(place_kernel, views, share),
        jax.ShapeDtypeStruct((1, channels, rows, part), F32),
        far, *back[:edge],
    )


def solution(mesh):
    in_specs = (
        P("view", None, ("group", "row"), None),
        P("depth", "view", ("group", "row"), None),
        P("view", "depth", ("group", "row"), None),
        P("view", "depth", ("group", "row"), None),
        P(None, "view", "depth", ("group", "row"), None),
    )
    out_specs = P("view", None, ("group", "row"), "depth")
    return jax.shard_map(
        per_device, mesh=mesh, in_specs=in_specs, out_specs=out_specs, check_vma=False
    )
```
